32 devices in a mesh: dp: 2 (over y), ctx: 4 (over x, core), tp: 4 (over z).
Axes of the slice: x: 2, y: 2, z: 4, core: 2. Of those that a mesh axis runs over, the one named last changes fastest.
Arguments:
- queries: bfloat16 [1024, 4096], P(('dp', 'ctx'), 'tp'), parts along dimension 0, may hold values from -6.5 to 6.5
- keys: bfloat16 [1024, 512], P(('dp', 'ctx'), 'tp'), parts along dimension 0, may hold values from -6.5 to 6.5
- values: bfloat16 [1024, 512], P(('dp', 'ctx'), 'tp'), parts along dimension 0, may hold values from -6 to 6
- out_weight: bfloat16 [4096, 2048], P('tp'), may hold values from -0.375 to 0.375
- norm_gain: float32 [2048], replicated, may hold values from 0.5 to 1.5
- expert_gate: bfloat16 [16, 2048, 384], P(('ctx', 'tp')), may hold values from -0.125 to 0.125
- expert_up: bfloat16 [16, 2048, 384], P(('ctx', 'tp')), may hold values from -0.125 to 0.125
- expert_down: bfloat16 [16, 384, 2048], P(('ctx', 'tp')), may hold values from -0.3125 to 0.3125
- expert_ids: int32 [1024, 8], P(('dp', 'ctx')), parts along dimension 0, may hold values from 0 to 15, as said below
- route_weights: float32 [1024, 8], P(('dp', 'ctx')), parts along dimension 0, may hold values from 0.05 to 1
Outputs:
- attended: bfloat16 [1024, 4096], P(('dp', 'ctx'), 'tp'), parts along dimension 0
- layer_out: bfloat16 [1024, 2048], P(('dp', 'ctx', 'tp')), parts along dimension 0
The draws below stay inside these ranges and needn't reach their ends.
There are 2 independent parts, one for each index of `dp`. The reference program is written for one: setup_inputs(seed, part) draws one part's arguments, and reference() takes and returns one part's arrays. A program takes and returns all parts, laid end to end along the dimension named above; an argument that names none is the same for every part. Nothing has to cross between parts.
Inputs may be any that keep to these rules, and one draw needn't show every extreme that they name: `expert_ids`: each row names 8 different experts. In each aligned block of 128 rows (the rows of one ctx index) every expert is named by at least 32 and at most 96 rows, and one expert is named by exactly 96 rows in every block.
All inputs are finite; a program needn't handle non-finite values.
Results may differ from the reference program's by a relative error of at most 0.02.
Values may be sent and summed in bfloat16 or wider, within the bound.
No kernel may reach another device: no remote copies, remote signals or barrier semaphores. Data moves between devices by JAX's collectives and lax.ppermute only.
A program may use at most 64 MiB of HBM per device.

```python
import jax
import jax.numpy as jnp
from jax import lax

D = 2048
QH = 32
KVH = 4
HEAD = 128
TOPK = 8
EFF = 384
BLK = 128
L = 512
EXPERTS = 16
CAP = 96
N_CTX = 4


def base_field(key, features):
    return jnp.clip(jax.random.normal(key, (L, features), jnp.float32), -6.0, 6.0)


def draw_queries(key, part):
    field = base_field(jax.random.fold_in(key, 11), QH * HEAD).reshape(L, QH, HEAD)
    return field.reshape(L, QH * HEAD).astype(jnp.bfloat16)


def draw_keys(key, part):
    field = base_field(jax.random.fold_in(key, 12), KVH * HEAD).reshape(L, KVH, HEAD)
    return field.reshape(L, KVH * HEAD).astype(jnp.bfloat16)


def route_block(key, hot_expert):
    base_load = BLK * TOPK // EXPERTS
    spread_load = CAP - base_load
    ranking = jax.random.permutation(jax.random.fold_in(key, 1), EXPERTS).astype(jnp.int32)
    ranking = jnp.where(jnp.arange(EXPERTS, dtype=jnp.int32) == hot_expert, -1, ranking)
    pairing = jnp.argsort(ranking, stable=True)
    moves = jax.random.randint(jax.random.fold_in(key, 2), (EXPERTS // 2,), 0, spread_load + 1)
    moves = moves.at[0].set(spread_load)
    loads = jnp.full((EXPERTS,), base_load, jnp.int32).at[pairing[0::2]].add(moves).at[pairing[1::2]].add(-moves)
    layout = jax.random.permutation(jax.random.fold_in(key, 3), EXPERTS).astype(jnp.int32)
    ends = jnp.cumsum(loads[layout])
    entries = jnp.arange(BLK * TOPK, dtype=jnp.int32)
    owner = jnp.sum((ends[None, :] <= entries[:, None]).astype(jnp.int32), axis=1)
    block_table = layout[owner].reshape(TOPK, BLK).T
    row_order = jax.random.permutation(jax.random.fold_in(key, 4), BLK)
    return block_table[row_order]


def draw_expert_ids(key, part):
    hot_expert = jax.random.randint(jax.random.fold_in(key, 21), (), 0, EXPERTS)
    block_keys = jax.random.split(jax.random.fold_in(key, 22), L // BLK)
    blocks = jax.vmap(lambda one_key: route_block(one_key, hot_expert))(block_keys)
    return blocks.reshape(L, TOPK).astype(jnp.int32)


def shard_levels(stream_key, extent, pieces, least, top_value):
    gain, own = 1.0, jax.random.fold_in(stream_key, 6)
    for position, blocks in pieces:
        heights = jnp.exp(jax.random.uniform(jax.random.fold_in(own, position), (blocks,), jnp.float32, least / len(pieces), top_value / len(pieces)))
        gain = gain * jnp.repeat(heights, extent[position] // blocks).reshape([-1 if axis == position else 1 for axis in range(len(extent))])
    return gain


def normal_values(stream_key, dims, scale, most, shards=(), kind=jnp.bfloat16):
    level = shard_levels(stream_key, dims, shards, -0.22, 0.18) if shards else 1.0
    result = jax.random.normal(stream_key, dims, jnp.float32) * scale * level
    return jnp.minimum(jnp.maximum(result, -most), most).astype(kind)


def setup_inputs(seed: int = 0, part: int = 0) -> dict:
    key_list = jax.random.split(jax.random.key(seed), 11)
    part_keys = jax.random.split(jax.random.fold_in(key_list[10], part), 11)
    queries = draw_queries(jax.random.fold_in(jax.random.fold_in(key_list[10], part), 71), part)
    keys = draw_keys(jax.random.fold_in(jax.random.fold_in(key_list[10], part), 71), part)
    values = normal_values(part_keys[2], (L, KVH * HEAD), 1.0, 6.0, ((0, 4), (1, 4)))
    out_weight = normal_values(key_list[3], (QH * HEAD, D), (QH * HEAD // 16) ** -0.5, 0.375, ((0, 4),))
    norm_gain = jnp.clip(1.0 + 0.1 * jax.random.normal(key_list[4], (D,), jnp.float32), 0.5, 1.5)
    expert_gate = normal_values(key_list[5], (EXPERTS, D, EFF), D ** -0.5, 0.125, ((0, 16),))
    expert_up = normal_values(key_list[6], (EXPERTS, D, EFF), D ** -0.5, 0.125, ((0, 16),))
    expert_down = normal_values(key_list[7], (EXPERTS, EFF, D), EFF ** -0.5, 0.3125, ((0, 16),))
    expert_ids = draw_expert_ids(jax.random.fold_in(jax.random.fold_in(key_list[10], part), 71), part)
    route_weights = jnp.clip(0.05 + 0.95 * jax.random.uniform(part_keys[9], (L, TOPK), jnp.float32) ** shard_levels(part_keys[9], (L, TOPK), ((0, 4),), -0.2, 0.2), 0.05, 1.0)
    return {"queries": queries, "keys": keys, "values": values, "out_weight": out_weight, "norm_gain": norm_gain, "expert_gate": expert_gate, "expert_up": expert_up, "expert_down": expert_down, "expert_ids": expert_ids, "route_weights": route_weights}


def head_attention(operands):
    q_head, k_head, v_head = operands
    scores = jnp.dot(q_head, k_head.T, preferred_element_type=jnp.float32) * HEAD ** (-0.5)
    positions = jnp.arange(L, dtype=jnp.int32)
    allowed = positions[None, :] <= positions[:, None]
    scores = jnp.where(allowed, scores, -jnp.inf)
    row_max = lax.optimization_barrier(jnp.max(scores, axis=1, keepdims=True))
    probs = jnp.exp(scores - row_max)
    row_total = lax.optimization_barrier(jnp.sum(probs, axis=1, keepdims=True))
    weighted = jnp.dot(probs.astype(jnp.bfloat16), v_head, preferred_element_type=jnp.float32)
    return (weighted / row_total).astype(jnp.bfloat16)

def reference(queries, keys, values, out_weight, norm_gain, expert_gate, expert_up, expert_down, expert_ids, route_weights):
    group_size = QH // KVH
    q_heads = queries.reshape(L, QH, HEAD).transpose(1, 0, 2)
    k_heads = jnp.repeat(keys.reshape(L, KVH, HEAD).transpose(1, 0, 2), group_size, axis=0)
    v_heads = jnp.repeat(values.reshape(L, KVH, HEAD).transpose(1, 0, 2), group_size, axis=0)
    attended_heads = lax.map(head_attention, (q_heads, k_heads, v_heads))
    attended = attended_heads.transpose(1, 0, 2).reshape(L, QH * HEAD)
    projected = jnp.dot(attended, out_weight, preferred_element_type=jnp.float32)
    normed = (projected * lax.rsqrt(lax.optimization_barrier(jnp.mean(projected * projected, axis=1, keepdims=True)) + 1e-06) * norm_gain).astype(jnp.bfloat16)
    share = route_weights / lax.optimization_barrier(jnp.sum(route_weights, axis=1, keepdims=True))
    flat_ids = expert_ids.reshape(-1).astype(jnp.int32)
    token_index = (jnp.arange(L * TOPK, dtype=jnp.int32) // TOPK).astype(jnp.int32)
    one_hot = (flat_ids[:, None] == jnp.arange(EXPERTS, dtype=jnp.int32)[None, :]).astype(jnp.int32)
    running = jnp.cumsum(one_hot, axis=0).astype(jnp.int32) - 1
    slot_index = lax.optimization_barrier(jnp.sum(running * one_hot, axis=1)).astype(jnp.int32)
    max_load = N_CTX * CAP
    slot_table = jnp.zeros((EXPERTS, max_load), jnp.int32).at[flat_ids, slot_index].set(token_index)

    def run_expert(operands):
        gate_weight, up_weight, down_weight, token_rows = operands
        inputs = normed[token_rows]
        gate_proj = jnp.dot(inputs, gate_weight, preferred_element_type=jnp.float32)
        up_proj = jnp.dot(inputs, up_weight, preferred_element_type=jnp.float32)
        activated = (jax.nn.silu(gate_proj) * up_proj).astype(jnp.bfloat16)
        return jnp.dot(activated, down_weight, preferred_element_type=jnp.float32).astype(jnp.bfloat16)
    expert_outs = lax.map(run_expert, (expert_gate, expert_up, expert_down, slot_table))
    assigned = expert_outs[flat_ids, slot_index].astype(jnp.float32).reshape(L, TOPK, D)
    expert_mix = lax.optimization_barrier(jnp.sum(assigned * share[:, :, None], axis=1))
    layer_out = (projected + expert_mix).astype(jnp.bfloat16)
    return (attended, layer_out)
```

```python
import math

import jax
import jax.numpy as jnp
from jax import lax
from jax.sharding import PartitionSpec as P

HEAD = 128


def rms_scale(proj_rows, norm_gain):
    inverse = lax.rsqrt(jnp.mean(proj_rows * proj_rows, axis=1, keepdims=True) + 1e-06)
    return (proj_rows * inverse * norm_gain).astype(jnp.bfloat16)


def routed_plan(
    queries,
    keys,
    values,
    out_weight,
    norm_gain,
    expert_gate,
    expert_up,
    expert_down,
    expert_ids,
    route_weights,
):
    ctx_count = lax.axis_size("ctx")
    tp_count = lax.axis_size("tp")
    ctx_index = lax.axis_index("ctx")
    tp_index = lax.axis_index("tp")
    block_rows = queries.shape[0]
    local_heads = queries.shape[1] // HEAD
    kv_local = keys.shape[1] // HEAD
    group_size = local_heads // kv_local
    query_grid = queries.reshape(block_rows, kv_local, group_size, HEAD)
    query_pos = ctx_index * block_rows + jnp.arange(block_rows, dtype=jnp.int32)
    last_query = ctx_index * block_rows + block_rows - 1
    score_scale = HEAD ** (-0.5)

    def key_step(state_now, key_part, value_part, first_key):
        running_max, row_total, accum = state_now
        key_count = key_part.shape[0]
        key_grid = key_part.reshape(key_count, kv_local, HEAD)
        value_grid = value_part.reshape(key_count, kv_local, HEAD)
        scores = (
            jnp.einsum("tkgd,ukd->kgtu", query_grid, key_grid, preferred_element_type=jnp.float32)
            * score_scale
        )
        key_pos = first_key + jnp.arange(key_count, dtype=jnp.int32)
        allowed = key_pos[None, :] <= query_pos[:, None]
        new_max = jnp.maximum(running_max, jnp.max(jnp.where(allowed, scores, -1e30), axis=3))
        key_weights = jnp.where(allowed, jnp.exp(scores - new_max[..., None]), 0.0)
        rescale = jnp.exp(running_max - new_max)
        row_total = row_total * rescale + jnp.sum(key_weights, axis=3)
        update = jnp.einsum(
            "kgtu,ukd->kgtd",
            key_weights.astype(jnp.bfloat16),
            value_grid,
            preferred_element_type=jnp.float32,
        )
        accum = accum * rescale[..., None] + update
        return (new_max, row_total, accum)

    initial = (
        jnp.full((kv_local, group_size, block_rows), -1e30, jnp.float32),
        jnp.zeros((kv_local, group_size, block_rows), jnp.float32),
        jnp.zeros((kv_local, group_size, block_rows, HEAD), jnp.float32),
    )
    running_state = initial
    key_rows = lax.all_gather(keys, "ctx", axis=0, tiled=True)
    value_rows = lax.all_gather(values, "ctx", axis=0, tiled=True)
    key_count = key_rows.shape[0]
    sub_rows = math.gcd(key_count, 512)

    def sub_step(partial_value, sub_index):
        offset = sub_index * sub_rows
        key_part = lax.dynamic_slice_in_dim(key_rows, offset, sub_rows, 0)
        value_part = lax.dynamic_slice_in_dim(value_rows, offset, sub_rows, 0)
        updated = lax.cond(
            offset <= last_query,
            lambda state_now: key_step(state_now, key_part, value_part, offset),
            lambda state_now: state_now,
            partial_value,
        )
        return (updated, None)

    running_state, unused = lax.scan(
        sub_step, running_state, jnp.arange(key_count // sub_rows, dtype=jnp.int32)
    )
    final_max, row_total, accum = running_state
    attended = (
        (accum / row_total[..., None])
        .transpose(2, 0, 1, 3)
        .reshape(block_rows, local_heads * HEAD)
        .astype(jnp.bfloat16)
    )
    own_proj = lax.psum_scatter(
        jnp.dot(attended, out_weight, preferred_element_type=jnp.float32).astype(jnp.bfloat16),
        "tp",
        scatter_dimension=0,
        tiled=True,
    ).astype(jnp.float32)
    normed = lax.all_gather(rms_scale(own_proj, norm_gain), "tp", axis=0, tiled=True)
    top_count = expert_ids.shape[1]
    capacity = block_rows * top_count // (ctx_count * tp_count) * 3 // 2
    slot_total = ctx_count * capacity
    is_mine = expert_ids % tp_count == tp_index
    target_ctx = expert_ids // tp_count
    flat_target = target_ctx.reshape(-1)
    flat_mine = is_mine.reshape(-1)
    to_target = (
        flat_target[:, None] == jnp.arange(ctx_count, dtype=jnp.int32)[None, :]
    ) & flat_mine[:, None]
    running = jnp.cumsum(to_target.astype(jnp.int32), axis=0) - 1
    position = jnp.sum(jnp.where(to_target, running, 0), axis=1)
    slot_id = jnp.where(flat_mine, flat_target * capacity + position, -1).reshape(
        block_rows, top_count
    )
    slot_match = slot_id[:, :, None] == jnp.arange(slot_total, dtype=jnp.int32)[None, None, :]
    dispatch_map = jnp.any(slot_match, axis=1).astype(jnp.bfloat16)
    outgoing = jnp.einsum(
        "ts,td->sd", dispatch_map, normed, preferred_element_type=jnp.float32
    ).astype(jnp.bfloat16)
    outgoing = outgoing.reshape(ctx_count, capacity, normed.shape[1])
    route_share = route_weights / jnp.sum(route_weights, axis=1, keepdims=True)
    mix_weights = jnp.sum(jnp.where(slot_match, route_share[:, :, None], 0.0), axis=1)
    mix_high = mix_weights.astype(jnp.bfloat16)
    mix_low = (mix_weights - mix_high.astype(jnp.float32)).astype(jnp.bfloat16)
    arrived = lax.all_to_all(outgoing, "ctx", split_axis=0, concat_axis=0, tiled=True)
    source_count, item_count, features = arrived.shape
    flattened = arrived.reshape(source_count * item_count, features)
    gate_proj = jnp.dot(flattened, expert_gate[0], preferred_element_type=jnp.float32)
    up_proj = jnp.dot(flattened, expert_up[0], preferred_element_type=jnp.float32)
    activated = (jax.nn.silu(gate_proj) * up_proj).astype(jnp.bfloat16)
    expert_out = jnp.dot(activated, expert_down[0], preferred_element_type=jnp.float32).astype(
        jnp.bfloat16
    )
    expert_out = expert_out.reshape(source_count, item_count, features)
    returned = lax.all_to_all(expert_out, "ctx", split_axis=0, concat_axis=0, tiled=True)
    returned_flat = returned.reshape(slot_total, returned.shape[2])
    high_part = jnp.dot(mix_high, returned_flat, preferred_element_type=jnp.float32)
    expert_mix = lax.psum_scatter(
        (high_part + jnp.dot(mix_low, returned_flat, preferred_element_type=jnp.float32)).astype(
            jnp.bfloat16
        ),
        "tp",
        scatter_dimension=0,
        tiled=True,
    ).astype(jnp.float32)
    layer_out = (own_proj + expert_mix).astype(jnp.bfloat16)
    return (attended, layer_out)


def swap(rows, axis, offset):
    count = lax.axis_size(axis)
    return lax.ppermute(rows, axis, [(i, i ^ offset) for i in range(count)])


def dense_plan(
    queries,
    keys,
    values,
    out_weight,
    norm_gain,
    expert_gate,
    expert_up,
    expert_down,
    expert_ids,
    route_weights,
):
    f32, bf16 = jnp.float32, jnp.bfloat16
    ctx_count = lax.axis_size("ctx")
    tp_count = lax.axis_size("tp")
    ctx_index = lax.axis_index("ctx")
    tp_index = lax.axis_index("tp")
    block_rows = queries.shape[0]
    local_heads = queries.shape[1] // HEAD
    kv_local = keys.shape[1] // HEAD
    group_size = local_heads // kv_local
    piece_rows = block_rows // tp_count
    features = out_weight.shape[1]
    expert_count = ctx_count * tp_count

    own_kv = jnp.stack([keys, values])
    kv = [own_kv] + [swap(own_kv, "ctx", d) for d in range(1, ctx_count)]

    share = route_weights / jnp.sum(route_weights, axis=1, keepdims=True)
    chosen = expert_ids[:, :, None] == jnp.arange(expert_count, dtype=jnp.int32)[None, None, :]
    mix = jnp.sum(jnp.where(chosen, share[:, :, None], 0.0), axis=1)
    mixes = [mix] + [swap(mix, "ctx", d) for d in range(1, ctx_count)]
    my_expert = ctx_index * tp_count + tp_index
    my_mix = [lax.dynamic_slice_in_dim(m, my_expert, 1, 1) for m in mixes]

    query_grid = queries.reshape(block_rows, kv_local, group_size, HEAD)
    key_grid = jnp.concatenate([b[0] for b in kv]).reshape(-1, kv_local, HEAD)
    value_grid = jnp.concatenate([b[1] for b in kv]).reshape(-1, kv_local, HEAD)
    row = jnp.arange(block_rows, dtype=jnp.int32)
    allowed = jnp.concatenate(
        [row[None, :] <= row[:, None]]
        + [
            jnp.broadcast_to((ctx_index ^ d) < ctx_index, (block_rows, block_rows))
            for d in range(1, ctx_count)
        ],
        axis=1,
    )
    scores = jnp.einsum(
        "tkgd,ukd->kgtu", query_grid, key_grid, preferred_element_type=f32
    ) * HEAD ** (-0.5)
    scores = jnp.where(allowed, scores, -1e30)
    weights = jnp.exp(scores - jnp.max(scores, axis=3, keepdims=True))
    total = jnp.sum(weights, axis=3, keepdims=True)
    accum = jnp.einsum(
        "kgtu,ukd->kgtd", weights.astype(bf16), value_grid, preferred_element_type=f32
    )
    attended = (
        (accum / total).transpose(2, 0, 1, 3).reshape(block_rows, local_heads * HEAD).astype(bf16)
    )

    partial = jnp.dot(attended, out_weight, preferred_element_type=f32).astype(bf16)

    def piece_of(d):
        return lax.dynamic_slice_in_dim(partial, (tp_index ^ d) * piece_rows, piece_rows, 0)

    own_proj = piece_of(0).astype(f32)
    for d in (2, 3, 1):
        own_proj = own_proj + swap(piece_of(d), "tp", d).astype(f32)
    normed = rms_scale(own_proj, norm_gain)

    def expert(tokens, mix_rows):
        gate_proj = jnp.dot(tokens, expert_gate[0], preferred_element_type=f32)
        up_proj = jnp.dot(tokens, expert_up[0], preferred_element_type=f32)
        activated = (jax.nn.silu(gate_proj) * up_proj).astype(bf16)
        return jnp.dot(activated, expert_down[0], preferred_element_type=f32) * mix_rows

    pieces = [normed] + [swap(normed, "tp", d) for d in (1, 2, 3)]
    sums = []
    for d, piece in enumerate(pieces):
        far = swap(piece, "ctx", 2)
        near = swap(jnp.stack([piece, far]), "ctx", 1)
        tokens = jnp.concatenate([piece, near[0], far, near[1]])
        row_start = (tp_index ^ d) * piece_rows
        mix_rows = jnp.concatenate(
            [lax.dynamic_slice_in_dim(m, row_start, piece_rows, 0) for m in my_mix]
        )
        out = expert(tokens, mix_rows).reshape(ctx_count, piece_rows, features)
        got = swap(jnp.stack([out[1], out[3]]).astype(bf16), "ctx", 1).astype(f32)
        far_sum = swap((out[2] + got[1]).astype(bf16), "ctx", 2).astype(f32)
        sums.append(out[0] + got[0] + far_sum)
    expert_mix = sums[0]
    for d in (2, 3, 1):
        expert_mix = expert_mix + swap(sums[d].astype(bf16), "tp", d).astype(f32)
    return (attended, (own_proj + expert_mix).astype(bf16))


def per_device(*arguments):
    ctx_count, tp_count = lax.axis_size("ctx"), lax.axis_size("tp")
    top_count = arguments[8].shape[1]
    if ctx_count == 4 and tp_count == 4 and ctx_count * tp_count <= 2 * top_count:
        return dense_plan(*arguments)
    return routed_plan(*arguments)


def solution(mesh):
    in_specs = (
        P(("dp", "ctx"), "tp"),
        P(("dp", "ctx"), "tp"),
        P(("dp", "ctx"), "tp"),
        P("tp", None),
        P(),
        P(("ctx", "tp"), None, None),
        P(("ctx", "tp"), None, None),
        P(("ctx", "tp"), None, None),
        P(("dp", "ctx"), None),
        P(("dp", "ctx"), None),
    )
    out_specs = (P(("dp", "ctx"), "tp"), P(("dp", "ctx", "tp"), None))
    return jax.shard_map(
        per_device, mesh=mesh, in_specs=in_specs, out_specs=out_specs, check_vma=False
    )
```

```python
import functools
import math

import jax
import jax.numpy as jnp
from jax import lax
from jax.experimental import pallas as pl
from jax.experimental.pallas import tpu as pltpu
from jax.sharding import PartitionSpec as P

HEAD = 128


def rms_scale(proj_rows, norm_gain):
    inverse = lax.rsqrt(jnp.mean(proj_rows * proj_rows, axis=1, keepdims=True) + 1e-06)
    return (proj_rows * inverse * norm_gain).astype(jnp.bfloat16)


def routed_plan(
    queries,
    keys,
    values,
    out_weight,
    norm_gain,
    expert_gate,
    expert_up,
    expert_down,
    expert_ids,
    route_weights,
):
    ctx_count = lax.axis_size("ctx")
    tp_count = lax.axis_size("tp")
    ctx_index = lax.axis_index("ctx")
    tp_index = lax.axis_index("tp")
    block_rows = queries.shape[0]
    local_heads = queries.shape[1] // HEAD
    kv_local = keys.shape[1] // HEAD
    group_size = local_heads // kv_local
    query_grid = queries.reshape(block_rows, kv_local, group_size, HEAD)
    query_pos = ctx_index * block_rows + jnp.arange(block_rows, dtype=jnp.int32)
    last_query = ctx_index * block_rows + block_rows - 1
    score_scale = HEAD ** (-0.5)

    def key_step(state_now, key_part, value_part, first_key):
        running_max, row_total, accum = state_now
        key_count = key_part.shape[0]
        key_grid = key_part.reshape(key_count, kv_local, HEAD)
        value_grid = value_part.reshape(key_count, kv_local, HEAD)
        scores = (
            jnp.einsum("tkgd,ukd->kgtu", query_grid, key_grid, preferred_element_type=jnp.float32)
            * score_scale
        )
        key_pos = first_key + jnp.arange(key_count, dtype=jnp.int32)
        allowed = key_pos[None, :] <= query_pos[:, None]
        new_max = jnp.maximum(running_max, jnp.max(jnp.where(allowed, scores, -1e30), axis=3))
        key_weights = jnp.where(allowed, jnp.exp(scores - new_max[..., None]), 0.0)
        rescale = jnp.exp(running_max - new_max)
        row_total = row_total * rescale + jnp.sum(key_weights, axis=3)
        update = jnp.einsum(
            "kgtu,ukd->kgtd",
            key_weights.astype(jnp.bfloat16),
            value_grid,
            preferred_element_type=jnp.float32,
        )
        accum = accum * rescale[..., None] + update
        return (new_max, row_total, accum)

    initial = (
        jnp.full((kv_local, group_size, block_rows), -1e30, jnp.float32),
        jnp.zeros((kv_local, group_size, block_rows), jnp.float32),
        jnp.zeros((kv_local, group_size, block_rows, HEAD), jnp.float32),
    )
    running_state = initial
    key_rows = lax.all_gather(keys, "ctx", axis=0, tiled=True)
    value_rows = lax.all_gather(values, "ctx", axis=0, tiled=True)
    key_count = key_rows.shape[0]
    sub_rows = math.gcd(key_count, 512)

    def sub_step(partial_value, sub_index):
        offset = sub_index * sub_rows
        key_part = lax.dynamic_slice_in_dim(key_rows, offset, sub_rows, 0)
        value_part = lax.dynamic_slice_in_dim(value_rows, offset, sub_rows, 0)
        updated = lax.cond(
            offset <= last_query,
            lambda state_now: key_step(state_now, key_part, value_part, offset),
            lambda state_now: state_now,
            partial_value,
        )
        return (updated, None)

    running_state, unused = lax.scan(
        sub_step, running_state, jnp.arange(key_count // sub_rows, dtype=jnp.int32)
    )
    final_max, row_total, accum = running_state
    attended = (
        (accum / row_total[..., None])
        .transpose(2, 0, 1, 3)
        .reshape(block_rows, local_heads * HEAD)
        .astype(jnp.bfloat16)
    )
    own_proj = lax.psum_scatter(
        jnp.dot(attended, out_weight, preferred_element_type=jnp.float32).astype(jnp.bfloat16),
        "tp",
        scatter_dimension=0,
        tiled=True,
    ).astype(jnp.float32)
    normed = lax.all_gather(rms_scale(own_proj, norm_gain), "tp", axis=0, tiled=True)
    top_count = expert_ids.shape[1]
    capacity = block_rows * top_count // (ctx_count * tp_count) * 3 // 2
    slot_total = ctx_count * capacity
    is_mine = expert_ids % tp_count == tp_index
    target_ctx = expert_ids // tp_count
    flat_target = target_ctx.reshape(-1)
    flat_mine = is_mine.reshape(-1)
    to_target = (
        flat_target[:, None] == jnp.arange(ctx_count, dtype=jnp.int32)[None, :]
    ) & flat_mine[:, None]
    running = jnp.cumsum(to_target.astype(jnp.int32), axis=0) - 1
    position = jnp.sum(jnp.where(to_target, running, 0), axis=1)
    slot_id = jnp.where(flat_mine, flat_target * capacity + position, -1).reshape(
        block_rows, top_count
    )
    slot_match = slot_id[:, :, None] == jnp.arange(slot_total, dtype=jnp.int32)[None, None, :]
    dispatch_map = jnp.any(slot_match, axis=1).astype(jnp.bfloat16)
    outgoing = jnp.einsum(
        "ts,td->sd", dispatch_map, normed, preferred_element_type=jnp.float32
    ).astype(jnp.bfloat16)
    outgoing = outgoing.reshape(ctx_count, capacity, normed.shape[1])
    route_share = route_weights / jnp.sum(route_weights, axis=1, keepdims=True)
    mix_weights = jnp.sum(jnp.where(slot_match, route_share[:, :, None], 0.0), axis=1)
    mix_high = mix_weights.astype(jnp.bfloat16)
    mix_low = (mix_weights - mix_high.astype(jnp.float32)).astype(jnp.bfloat16)
    arrived = lax.all_to_all(outgoing, "ctx", split_axis=0, concat_axis=0, tiled=True)
    source_count, item_count, features = arrived.shape
    flattened = arrived.reshape(source_count * item_count, features)
    gate_proj = jnp.dot(flattened, expert_gate[0], preferred_element_type=jnp.float32)
    up_proj = jnp.dot(flattened, expert_up[0], preferred_element_type=jnp.float32)
    activated = (jax.nn.silu(gate_proj) * up_proj).astype(jnp.bfloat16)
    expert_out = jnp.dot(activated, expert_down[0], preferred_element_type=jnp.float32).astype(
        jnp.bfloat16
    )
    expert_out = expert_out.reshape(source_count, item_count, features)
    returned = lax.all_to_all(expert_out, "ctx", split_axis=0, concat_axis=0, tiled=True)
    returned_flat = returned.reshape(slot_total, returned.shape[2])
    high_part = jnp.dot(mix_high, returned_flat, preferred_element_type=jnp.float32)
    expert_mix = lax.psum_scatter(
        (high_part + jnp.dot(mix_low, returned_flat, preferred_element_type=jnp.float32)).astype(
            jnp.bfloat16
        ),
        "tp",
        scatter_dimension=0,
        tiled=True,
    ).astype(jnp.float32)
    layer_out = (own_proj + expert_mix).astype(jnp.bfloat16)
    return (attended, layer_out)


F32, BF16 = jnp.float32, jnp.bfloat16
VMEM_SPEC = pl.BlockSpec(memory_space=pltpu.VMEM)


def swap(rows, axis, offset):
    count = lax.axis_size(axis)
    return lax.ppermute(rows, axis, [(i, i ^ offset) for i in range(count)])


def call(kernel, outs, operands, scratch=(), flops=0, moved=0, limit=32 << 20):
    return pl.pallas_call(
        kernel,
        out_shape=outs,
        in_specs=[VMEM_SPEC] * len(operands),
        out_specs=[VMEM_SPEC] * len(outs),
        scratch_shapes=scratch,
        compiler_params=pltpu.CompilerParams(vmem_limit_bytes=limit),
        cost_estimate=pl.CostEstimate(flops=flops, bytes_accessed=moved, transcendentals=0),
    )(*operands)


def attend_kernel(tp_count, q_ref, own_ref, kv1_ref, kv2_ref, kv3_ref, w_ref, att_ref, *piece_refs):
    ctx_index, tp_index = lax.axis_index("ctx"), lax.axis_index("tp")
    block_rows = q_ref.shape[0]
    heads = q_ref.shape[1] // HEAD
    kv_local = own_ref.shape[2] // HEAD
    group_size = heads // kv_local
    blocks = (own_ref, kv1_ref, kv2_ref, kv3_ref)
    row = lax.broadcasted_iota(jnp.int32, (block_rows, block_rows), 0)
    col = lax.broadcasted_iota(jnp.int32, (block_rows, block_rows), 1)
    low = jnp.where(col <= row, 0.0, -1e30)
    masks = [low] + [
        jnp.where((ctx_index ^ d) < ctx_index, 0.0, -1e30) * jnp.ones_like(low)
        for d in range(1, len(blocks))
    ]
    mask = jnp.concatenate(masks, axis=1)
    for g in range(kv_local):
        lanes = slice(g * HEAD, (g + 1) * HEAD)
        key_rows = jnp.concatenate([b[0, :, lanes] for b in blocks], axis=0)
        value_rows = jnp.concatenate([b[1, :, lanes] for b in blocks], axis=0)
        for j in range(group_size):
            h = g * group_size + j
            q = q_ref[:, h * HEAD : (h + 1) * HEAD]
            scores = lax.dot_general(
                q, key_rows, (((1,), (1,)), ((), ())), preferred_element_type=F32
            )
            scores = scores * HEAD ** (-0.5) + mask
            weights = jnp.exp(scores - jnp.max(scores, axis=1, keepdims=True))
            total = jnp.sum(weights, axis=1, keepdims=True)
            accum = jnp.dot(weights.astype(BF16), value_rows, preferred_element_type=F32)
            att_ref[:, h * HEAD : (h + 1) * HEAD] = (accum / total).astype(BF16)
    piece_rows = block_rows // tp_count
    scratch = piece_refs[-1]
    scratch[...] = jnp.dot(att_ref[...], w_ref[...], preferred_element_type=F32)
    for d in range(tp_count):
        start = pl.multiple_of((tp_index ^ d) * piece_rows, piece_rows)
        piece_refs[d][...] = scratch[pl.ds(start, piece_rows), :].astype(piece_refs[d].dtype)


def norm_kernel(gain_ref, own_ref, *refs):
    parts, (proj_ref, normed_ref) = refs[:-2], refs[-2:]
    proj = own_ref[...]
    for part in parts:
        proj = proj + part[...].astype(F32)
    proj_ref[...] = proj
    inverse = lax.rsqrt(jnp.mean(proj * proj, axis=1, keepdims=True) + 1e-06)
    normed_ref[...] = (proj * inverse * gain_ref[...]).astype(BF16)


def expert_kernel(
    offset, own_ref, far_ref, near_ref, mix_ref, gate_ref, up_ref, down_ref, keep_ref, send_ref
):
    tp_index = lax.axis_index("tp")
    rows = own_ref.shape[0]
    tokens = jnp.concatenate([own_ref[...], far_ref[...], near_ref[0], near_ref[1]], axis=0)
    gate_proj = jnp.dot(tokens, gate_ref[0], preferred_element_type=F32)
    up_proj = jnp.dot(tokens, up_ref[0], preferred_element_type=F32)
    activated = (gate_proj / (1.0 + jnp.exp(-gate_proj)) * up_proj).astype(BF16)
    out = jnp.dot(activated, down_ref[0], preferred_element_type=F32) * mix_ref[tp_index ^ offset]
    keep_ref[0] = out[:rows]
    keep_ref[1] = out[rows : 2 * rows]
    send_ref[0] = out[2 * rows : 3 * rows].astype(BF16)
    send_ref[1] = out[3 * rows :].astype(BF16)


def dense_plan(
    queries,
    keys,
    values,
    out_weight,
    norm_gain,
    expert_gate,
    expert_up,
    expert_down,
    expert_ids,
    route_weights,
):
    ctx_count = lax.axis_size("ctx")
    tp_count = lax.axis_size("tp")
    ctx_index = lax.axis_index("ctx")
    tp_index = lax.axis_index("tp")
    block_rows, width = queries.shape
    piece_rows = block_rows // tp_count
    features = out_weight.shape[1]

    own_kv = jnp.stack([keys, values])
    kv = [own_kv] + [swap(own_kv, "ctx", d) for d in range(1, ctx_count)]

    piece = jax.ShapeDtypeStruct((piece_rows, features), BF16)
    piece32 = jax.ShapeDtypeStruct((piece_rows, features), F32)
    attended, *partials = call(
        functools.partial(attend_kernel, tp_count),
        [jax.ShapeDtypeStruct((block_rows, width), BF16), piece32] + [piece] * (tp_count - 1),
        (queries, *kv, out_weight),
        scratch=[pltpu.VMEM((block_rows, features), F32)],
        flops=2 * block_rows * width * features + 4 * block_rows * block_rows * ctx_count * width,
        moved=out_weight.size * 2,
    )
    arrived = [swap(partials[d], "tp", d) for d in (2, 3, 1)]

    route_weights, expert_ids, _ = lax.optimization_barrier((route_weights, expert_ids, attended))
    share = route_weights / jnp.sum(route_weights, axis=1, keepdims=True)
    mixes = []
    for d in (0, 2, 1, 3):
        expert = (ctx_index ^ d) * tp_count + tp_index
        mix = jnp.sum(jnp.where(expert_ids == expert, share, 0.0), axis=1)
        mixes.append(swap(mix, "ctx", d) if d else mix)
    mix = jnp.stack(mixes).reshape(ctx_count, tp_count, piece_rows)
    mix = mix.transpose(1, 0, 2).reshape(tp_count, ctx_count * piece_rows, 1)

    own_proj, normed = call(
        norm_kernel, [piece32, piece], (norm_gain.reshape(1, features), partials[0], *arrived)
    )

    pieces = {0: normed}
    for d in (2, 3, 1):
        pieces[d] = swap(normed, "tp", d)
    sums = {}
    for d in (0, 1, 2, 3):
        far = swap(pieces[d], "ctx", 2)
        near = swap(jnp.stack([pieces[d], far]), "ctx", 1)
        keep, send = call(
            functools.partial(expert_kernel, d),
            [
                jax.ShapeDtypeStruct((2, piece_rows, features), F32),
                jax.ShapeDtypeStruct((2, piece_rows, features), BF16),
            ],
            (pieces[d], far, near, mix, expert_gate, expert_up, expert_down),
            flops=6 * ctx_count * piece_rows * features * expert_gate.shape[2],
            moved=3 * expert_gate.size * 2,
        )
        got = swap(send, "ctx", 1).astype(F32)
        far_sum = swap((keep[1] + got[1]).astype(BF16), "ctx", 2).astype(F32)
        sums[d] = keep[0] + got[0] + far_sum
    expert_mix = sums[0]
    for d in (1, 2, 3):
        expert_mix = expert_mix + swap(sums[d].astype(BF16), "tp", d).astype(F32)
    return (attended, (own_proj + expert_mix).astype(BF16))


def per_device(*arguments):
    ctx_count, tp_count = lax.axis_size("ctx"), lax.axis_size("tp")
    top_count = arguments[8].shape[1]
    if ctx_count == 4 and tp_count == 4 and ctx_count * tp_count <= 2 * top_count:
        return dense_plan(*arguments)
    return routed_plan(*arguments)


def solution(mesh):
    in_specs = (
        P(("dp", "ctx"), "tp"),
        P(("dp", "ctx"), "tp"),
        P(("dp", "ctx"), "tp"),
        P("tp", None),
        P(),
        P(("ctx", "tp"), None, None),
        P(("ctx", "tp"), None, None),
        P(("ctx", "tp"), None, None),
        P(("dp", "ctx"), None),
        P(("dp", "ctx"), None),
    )
    out_specs = (P(("dp", "ctx"), "tp"), P(("dp", "ctx", "tp"), None))
    return jax.shard_map(
        per_device, mesh=mesh, in_specs=in_specs, out_specs=out_specs, check_vma=False
    )
```

```python
import functools
import math

import jax
import jax.numpy as jnp
from jax import lax
from jax.experimental import pallas as pl
from jax.experimental.pallas import tpu as pltpu
from jax.sharding import PartitionSpec as P

HEAD = 128


def rms_scale(proj_rows, norm_gain):
    inverse = lax.rsqrt(jnp.mean(proj_rows * proj_rows, axis=1, keepdims=True) + 1e-06)
    return (proj_rows * inverse * norm_gain).astype(jnp.bfloat16)


def routed_plan(
    queries,
    keys,
    values,
    out_weight,
    norm_gain,
    expert_gate,
    expert_up,
    expert_down,
    expert_ids,
    route_weights,
):
    ctx_count = lax.axis_size("ctx")
    tp_count = lax.axis_size("tp")
    ctx_index = lax.axis_index("ctx")
    tp_index = lax.axis_index("tp")
    block_rows = queries.shape[0]
    local_heads = queries.shape[1] // HEAD
    kv_local = keys.shape[1] // HEAD
    group_size = local_heads // kv_local
    query_grid = queries.reshape(block_rows, kv_local, group_size, HEAD)
    query_pos = ctx_index * block_rows + jnp.arange(block_rows, dtype=jnp.int32)
    last_query = ctx_index * block_rows + block_rows - 1
    score_scale = HEAD ** (-0.5)

    def key_step(state_now, key_part, value_part, first_key):
        running_max, row_total, accum = state_now
        key_count = key_part.shape[0]
        key_grid = key_part.reshape(key_count, kv_local, HEAD)
        value_grid = value_part.reshape(key_count, kv_local, HEAD)
        scores = (
            jnp.einsum("tkgd,ukd->kgtu", query_grid, key_grid, preferred_element_type=jnp.float32)
            * score_scale
        )
        key_pos = first_key + jnp.arange(key_count, dtype=jnp.int32)
        allowed = key_pos[None, :] <= query_pos[:, None]
        new_max = jnp.maximum(running_max, jnp.max(jnp.where(allowed, scores, -1e30), axis=3))
        key_weights = jnp.where(allowed, jnp.exp(scores - new_max[..., None]), 0.0)
        rescale = jnp.exp(running_max - new_max)
        row_total = row_total * rescale + jnp.sum(key_weights, axis=3)
        update = jnp.einsum(
            "kgtu,ukd->kgtd",
            key_weights.astype(jnp.bfloat16),
            value_grid,
            preferred_element_type=jnp.float32,
        )
        accum = accum * rescale[..., None] + update
        return (new_max, row_total, accum)

    initial = (
        jnp.full((kv_local, group_size, block_rows), -1e30, jnp.float32),
        jnp.zeros((kv_local, group_size, block_rows), jnp.float32),
        jnp.zeros((kv_local, group_size, block_rows, HEAD), jnp.float32),
    )
    running_state = initial
    key_rows = lax.all_gather(keys, "ctx", axis=0, tiled=True)
    value_rows = lax.all_gather(values, "ctx", axis=0, tiled=True)
    key_count = key_rows.shape[0]
    sub_rows = math.gcd(key_count, 512)

    def sub_step(partial_value, sub_index):
        offset = sub_index * sub_rows
        key_part = lax.dynamic_slice_in_dim(key_rows, offset, sub_rows, 0)
        value_part = lax.dynamic_slice_in_dim(value_rows, offset, sub_rows, 0)
        updated = lax.cond(
            offset <= last_query,
            lambda state_now: key_step(state_now, key_part, value_part, offset),
            lambda state_now: state_now,
            partial_value,
        )
        return (updated, None)

    running_state, unused = lax.scan(
        sub_step, running_state, jnp.arange(key_count // sub_rows, dtype=jnp.int32)
    )
    final_max, row_total, accum = running_state
    attended = (
        (accum / row_total[..., None])
        .transpose(2, 0, 1, 3)
        .reshape(block_rows, local_heads * HEAD)
        .astype(jnp.bfloat16)
    )
    own_proj = lax.psum_scatter(
        jnp.dot(attended, out_weight, preferred_element_type=jnp.float32).astype(jnp.bfloat16),
        "tp",
        scatter_dimension=0,
        tiled=True,
    ).astype(jnp.float32)
    normed = lax.all_gather(rms_scale(own_proj, norm_gain), "tp", axis=0, tiled=True)
    top_count = expert_ids.shape[1]
    capacity = block_rows * top_count // (ctx_count * tp_count) * 3 // 2
    slot_total = ctx_count * capacity
    is_mine = expert_ids % tp_count == tp_index
    target_ctx = expert_ids // tp_count
    flat_target = target_ctx.reshape(-1)
    flat_mine = is_mine.reshape(-1)
    to_target = (
        flat_target[:, None] == jnp.arange(ctx_count, dtype=jnp.int32)[None, :]
    ) & flat_mine[:, None]
    running = jnp.cumsum(to_target.astype(jnp.int32), axis=0) - 1
    position = jnp.sum(jnp.where(to_target, running, 0), axis=1)
    slot_id = jnp.where(flat_mine, flat_target * capacity + position, -1).reshape(
        block_rows, top_count
    )
    slot_match = slot_id[:, :, None] == jnp.arange(slot_total, dtype=jnp.int32)[None, None, :]
    dispatch_map = jnp.any(slot_match, axis=1).astype(jnp.bfloat16)
    outgoing = jnp.einsum(
        "ts,td->sd", dispatch_map, normed, preferred_element_type=jnp.float32
    ).astype(jnp.bfloat16)
    outgoing = outgoing.reshape(ctx_count, capacity, normed.shape[1])
    route_share = route_weights / jnp.sum(route_weights, axis=1, keepdims=True)
    mix_weights = jnp.sum(jnp.where(slot_match, route_share[:, :, None], 0.0), axis=1)
    mix_high = mix_weights.astype(jnp.bfloat16)
    mix_low = (mix_weights - mix_high.astype(jnp.float32)).astype(jnp.bfloat16)
    arrived = lax.all_to_all(outgoing, "ctx", split_axis=0, concat_axis=0, tiled=True)
    source_count, item_count, features = arrived.shape
    flattened = arrived.reshape(source_count * item_count, features)
    gate_proj = jnp.dot(flattened, expert_gate[0], preferred_element_type=jnp.float32)
    up_proj = jnp.dot(flattened, expert_up[0], preferred_element_type=jnp.float32)
    activated = (jax.nn.silu(gate_proj) * up_proj).astype(jnp.bfloat16)
    expert_out = jnp.dot(activated, expert_down[0], preferred_element_type=jnp.float32).astype(
        jnp.bfloat16
    )
    expert_out = expert_out.reshape(source_count, item_count, features)
    returned = lax.all_to_all(expert_out, "ctx", split_axis=0, concat_axis=0, tiled=True)
    returned_flat = returned.reshape(slot_total, returned.shape[2])
    high_part = jnp.dot(mix_high, returned_flat, preferred_element_type=jnp.float32)
    expert_mix = lax.psum_scatter(
        (high_part + jnp.dot(mix_low, returned_flat, preferred_element_type=jnp.float32)).astype(
            jnp.bfloat16
        ),
        "tp",
        scatter_dimension=0,
        tiled=True,
    ).astype(jnp.float32)
    layer_out = (own_proj + expert_mix).astype(jnp.bfloat16)
    return (attended, layer_out)


F32, BF16 = jnp.float32, jnp.bfloat16
VMEM_SPEC = pl.BlockSpec(memory_space=pltpu.VMEM)
HBM_SPEC = pl.BlockSpec(memory_space=pltpu.HBM)
HIDDEN_SCORE = -1e30
MIB = 1 << 20


def swap(rows, axis, offset):
    count = lax.axis_size(axis)
    return lax.ppermute(rows, axis, [(i, i ^ offset) for i in range(count)])


def call(kernel, outs, operands, scratch=(), flops=0, moved=0, limit=16 * MIB, from_hbm=0):
    operands = [
        pltpu.with_memory_space_constraint(x, pltpu.HBM) if i < from_hbm else x
        for i, x in enumerate(operands)
    ]
    return pl.pallas_call(
        kernel,
        out_shape=outs,
        in_specs=[HBM_SPEC] * from_hbm + [VMEM_SPEC] * (len(operands) - from_hbm),
        out_specs=[VMEM_SPEC] * len(outs),
        scratch_shapes=scratch,
        compiler_params=pltpu.CompilerParams(vmem_limit_bytes=limit),
        cost_estimate=pl.CostEstimate(flops=1024, bytes_accessed=1024, transcendentals=0),
    )(*operands)


def own_block_kernel(tp_count, *refs):
    *sources, w_source = refs[:6]
    w_ref, q_ref, max_ref, total_ref, acc_ref, *mix_refs = refs[6:-6]
    k_ref, v_ref, ids_ref, weights_ref, arrived, w_arrived = refs[-6:]
    targets = (q_ref, k_ref, v_ref, ids_ref, weights_ref)
    copies = [
        pltpu.make_async_copy(source, target, arrived.at[i])
        for i, (source, target) in enumerate(zip(sources, targets))
    ]
    chunks = w_arrived.shape[0]
    depth = w_ref.shape[0] // chunks
    w_copies = [
        pltpu.make_async_copy(
            w_source.at[pl.ds(i * depth, depth)], w_ref.at[pl.ds(i * depth, depth)], w_arrived.at[i]
        )
        for i in range(chunks)
    ]
    for copy in copies + w_copies:
        copy.start()
    for copy in copies:
        copy.wait()
    ctx_index, tp_index = lax.axis_index("ctx"), lax.axis_index("tp")
    block_rows = q_ref.shape[0]
    kv_local = k_ref.shape[1] // HEAD
    group_size = q_ref.shape[1] // k_ref.shape[1]
    row = lax.broadcasted_iota(jnp.int32, (block_rows, block_rows), 0)
    col = lax.broadcasted_iota(jnp.int32, (block_rows, block_rows), 1)
    for g in range(kv_local):
        key_rows = k_ref[:, g * HEAD : (g + 1) * HEAD]
        value_rows = v_ref[:, g * HEAD : (g + 1) * HEAD]
        for h in range(g * group_size, (g + 1) * group_size):
            lanes = slice(h * HEAD, (h + 1) * HEAD)
            scores = lax.dot_general(
                q_ref[:, lanes], key_rows, (((1,), (1,)), ((), ())), preferred_element_type=F32
            )
            scores = jnp.where(col <= row, scores * HEAD ** (-0.5), HIDDEN_SCORE)
            top = jnp.max(scores, axis=1, keepdims=True)
            weights = jnp.exp(scores - top)
            max_ref[:, h : h + 1] = top
            total_ref[:, h : h + 1] = jnp.sum(weights, axis=1, keepdims=True)
            acc_ref[:, lanes] = jnp.dot(weights.astype(BF16), value_rows, preferred_element_type=F32)
    share = weights_ref[...] / jnp.sum(weights_ref[...], axis=0, keepdims=True)
    for d, mix_ref in enumerate(mix_refs):
        expert = (ctx_index ^ d) * tp_count + tp_index
        mix_ref[...] = jnp.sum(jnp.where(ids_ref[...] == expert, share, 0.0), axis=0, keepdims=True)
    for copy in w_copies:
        copy.wait()


def other_blocks_kernel(tp_count, others, *refs):
    w_ref, q_ref, max_ref, total_ref, acc_ref = refs[:5]
    k_refs, v_refs = refs[5 : 5 + others], refs[5 + others : 5 + 2 * others]
    att_ref, *piece_refs = refs[5 + 2 * others : -1]
    scratch = refs[-1]
    ctx_index, tp_index = lax.axis_index("ctx"), lax.axis_index("tp")
    block_rows = q_ref.shape[0]
    kv_local = k_refs[0].shape[1] // HEAD
    group_size = q_ref.shape[1] // k_refs[0].shape[1]
    bias = jnp.concatenate(
        [
            jnp.full((1, block_rows), jnp.where((ctx_index ^ d) < ctx_index, 0.0, HIDDEN_SCORE))
            for d in range(1, others + 1)
        ],
        axis=1,
    )
    for g in range(kv_local):
        kv_lanes = slice(g * HEAD, (g + 1) * HEAD)
        key_rows = jnp.concatenate([r[:, kv_lanes] for r in k_refs], axis=0)
        value_rows = jnp.concatenate([r[:, kv_lanes] for r in v_refs], axis=0)
        for h in range(g * group_size, (g + 1) * group_size):
            lanes = slice(h * HEAD, (h + 1) * HEAD)
            scores = lax.dot_general(
                q_ref[:, lanes], key_rows, (((1,), (1,)), ((), ())), preferred_element_type=F32
            )
            scores = scores * HEAD ** (-0.5) + bias
            old = max_ref[:, h : h + 1]
            top = jnp.maximum(old, jnp.max(scores, axis=1, keepdims=True))
            weights = jnp.exp(scores - top)
            rescale = jnp.exp(old - top)
            total = total_ref[:, h : h + 1] * rescale + jnp.sum(weights, axis=1, keepdims=True)
            accum = acc_ref[:, lanes] * rescale + jnp.dot(
                weights.astype(BF16), value_rows, preferred_element_type=F32
            )
            att_ref[:, lanes] = (accum * (1.0 / total)).astype(BF16)
    piece_rows = block_rows // tp_count
    scratch[...] = jnp.dot(att_ref[...], w_ref[...], preferred_element_type=F32)
    for d in range(tp_count):
        start = pl.multiple_of((tp_index ^ d) * piece_rows, piece_rows)
        piece_refs[d][...] = scratch[pl.ds(start, piece_rows), :].astype(piece_refs[d].dtype)


def norm_kernel(ctx_count, gain_ref, *refs):
    mix_refs, parts = refs[:ctx_count], refs[ctx_count:-6]
    proj_ref, normed_ref, column_ref = refs[-3:]
    proj = parts[0][...]
    for part in parts[1:]:
        proj = proj + part[...].astype(F32)
    proj_ref[...] = proj
    inverse = lax.rsqrt(jnp.mean(proj * proj, axis=1, keepdims=True) + 1e-06)
    normed_ref[...] = (proj * inverse * gain_ref[...]).astype(BF16)
    column_ref[...] = jnp.concatenate([r[...] for r in mix_refs], axis=0).T


def expert_kernel(offsets, *refs):
    count = len(refs) // 2 - 2
    token_refs, out_refs = refs[:count], refs[-count:]
    column_ref, gate_ref, up_ref, down_ref = refs[count : count + 4]
    rows = token_refs[0].shape[0]
    tokens = jnp.concatenate([r[...] for r in token_refs], axis=0)
    gate_proj = jnp.dot(tokens, gate_ref[0], preferred_element_type=F32)
    up_proj = jnp.dot(tokens, up_ref[0], preferred_element_type=F32)
    activated = (gate_proj / (1.0 + jnp.exp(-gate_proj)) * up_proj).astype(BF16)
    out = jnp.dot(activated, down_ref[0], preferred_element_type=F32)
    partners = count // len(offsets)
    for i, out_ref in enumerate(out_refs):
        start = pl.multiple_of((lax.axis_index("tp") ^ offsets[i // partners]) * rows, rows)
        mix = column_ref[pl.ds(start, rows), i % partners : i % partners + 1]
        out_ref[...] = (out[i * rows : (i + 1) * rows] * mix).astype(out_ref.dtype)


def sum_kernel(*refs):
    total = refs[0][...].astype(F32)
    for ref in refs[1:-1]:
        total = total + ref[...].astype(F32)
    refs[-1][...] = total.astype(refs[-1].dtype)


def dense_plan(
    queries,
    keys,
    values,
    out_weight,
    norm_gain,
    expert_gate,
    expert_up,
    expert_down,
    expert_ids,
    route_weights,
):
    ctx_count = lax.axis_size("ctx")
    tp_count = lax.axis_size("tp")
    block_rows, width = queries.shape
    heads = width // HEAD
    piece_rows = block_rows // tp_count
    features = out_weight.shape[1]
    shape = jax.ShapeDtypeStruct

    far_k, far_v = swap(keys, "ctx", 2), swap(values, "ctx", 2)
    near_k, near_v = swap(keys, "ctx", 1), swap(values, "ctx", 1)
    projection, queries, top, total, accum, *mixes = call(
        functools.partial(own_block_kernel, tp_count),
        [shape(out_weight.shape, BF16), shape((block_rows, width), BF16)]
        + [shape((block_rows, heads), F32)] * 2
        + [shape((block_rows, width), F32)]
        + [shape((1, block_rows), F32)] * ctx_count,
        (queries, keys, values, expert_ids.T, route_weights.T, out_weight),
        scratch=[
            pltpu.VMEM(keys.shape, BF16),
            pltpu.VMEM(values.shape, BF16),
            pltpu.VMEM(expert_ids.T.shape, jnp.int32),
            pltpu.VMEM(route_weights.T.shape, F32),
            pltpu.SemaphoreType.DMA((5,)),
            pltpu.SemaphoreType.DMA((4,)),
        ],
        flops=4 * block_rows * block_rows * width,
        moved=queries.size * 6,
        from_hbm=6,
    )
    far_k, far_v, top = lax.optimization_barrier((far_k, far_v, top))
    ks = [near_k, far_k, swap(far_k, "ctx", 1)]
    vs = [near_v, far_v, swap(far_v, "ctx", 1)]
    piece = shape((piece_rows, features), BF16)
    piece32 = shape((piece_rows, features), F32)
    attended, *partials = call(
        functools.partial(other_blocks_kernel, tp_count, ctx_count - 1),
        [shape((block_rows, width), BF16), piece32] + [piece] * (tp_count - 1),
        (projection, queries, top, total, accum, *ks, *vs),
        scratch=[pltpu.VMEM((block_rows, features), F32)],
        flops=2 * block_rows * width * features + 4 * block_rows * block_rows * ctx_count * width,
        moved=out_weight.size * 2,
    )

    arrived = [swap(partials[d], "tp", d) for d in (2, 3, 1)]
    mixes = mixes[:1] + [swap(mixes[d], "ctx", d) for d in range(1, ctx_count)]
    own_proj, normed, columns = call(
        functools.partial(norm_kernel, ctx_count),
        [piece32, piece, shape((block_rows, ctx_count), F32)],
        (
            norm_gain.reshape(1, features),
            *mixes,
            partials[0],
            *arrived,
            expert_gate,
            expert_up,
            expert_down,
        ),
        flops=8 * piece_rows * features,
    )

    def after(values, *earlier):
        return lax.optimization_barrier((tuple(values), earlier))[0]

    def work(group, tokens):
        found = call(
            functools.partial(expert_kernel, group),
            [piece32, piece, piece32, piece] * len(group),
            (*tokens, columns, expert_gate, expert_up, expert_down),
            flops=6 * ctx_count * piece_rows * features * expert_gate.shape[2],
            moved=3 * expert_gate.size * 2,
        )
        return [found[4 * i : 4 * i + 4] for i in range(len(group))]

    def spread(rows, far):
        return [rows, swap(rows, "ctx", 1), far, swap(far, "ctx", 1)]

    def gather_results(out):
        out0, out1, out2, out3 = out
        got0, got2 = swap(out1, "ctx", 1), swap(out3, "ctx", 1)
        (far_part,) = call(sum_kernel, [piece], (out2, got2))
        return [out0, got0, far_part]

    def send_back(parts, d):
        out0, got0, far_part = parts
        parts = [out0, got0, swap(far_part, "ctx", 2)]
        if not d:
            return parts
        (tp_part,) = call(sum_kernel, [piece], parts)
        return [swap(tp_part, "tp", d)]

    rows2, rows1 = swap(normed, "tp", 2), swap(normed, "tp", 1)
    far0 = swap(normed, "ctx", 2)
    far1 = swap(rows1, "ctx", 2)
    far2 = swap(rows2, "ctx", 2)
    rows3 = swap(rows2, "tp", 1)
    rows0, far0, rows1, far1 = after((normed, far0, rows1, far1), rows2)
    tokens = spread(rows0, far0) + spread(rows1, far1)
    far3 = swap(rows3, "ctx", 2)
    tokens = after(tokens, rows3, far2)
    out0, out1 = work((0, 1), tokens)
    parts1, parts0 = gather_results(out1), gather_results(out0)
    rows2, far2, rows3, far3 = after((rows2, far2, rows3, far3), out0[0])
    tokens = spread(rows2, far2) + spread(rows3, far3)
    tokens = after(tokens, parts1[2], parts0[2])
    back1 = swap(parts1[2], "ctx", 2)
    out2, out3 = work((2, 3), tokens)
    (tp1,) = call(sum_kernel, [piece], (*parts1[:2], back1))
    ret1 = swap(tp1, "tp", 1)
    parts2, parts3 = gather_results(out2), gather_results(out3)
    back2, back3 = swap(parts2[2], "ctx", 2), swap(parts3[2], "ctx", 2)
    (tp2,) = call(sum_kernel, [piece], (*parts2[:2], *after((back2,), ret1)))
    (tp3,) = call(sum_kernel, [piece], (*parts3[:2], back3))
    results = [own_proj, ret1, swap(tp2, "tp", 2), swap(tp3, "tp", 3)]
    parts0 = after(parts0, back3)
    results += send_back(parts0, 0)
    (layer_out,) = call(sum_kernel, [piece], results)
    return (attended, layer_out)


def per_device(*arguments):
    ctx_count, tp_count = lax.axis_size("ctx"), lax.axis_size("tp")
    top_count = arguments[8].shape[1]
    if ctx_count == 4 and tp_count == 4 and ctx_count * tp_count <= 2 * top_count:
        return dense_plan(*arguments)
    return routed_plan(*arguments)


def solution(mesh):
    in_specs = (
        P(("dp", "ctx"), "tp"),
        P(("dp", "ctx"), "tp"),
        P(("dp", "ctx"), "tp"),
        P("tp", None),
        P(),
        P(("ctx", "tp"), None, None),
        P(("ctx", "tp"), None, None),
        P(("ctx", "tp"), None, None),
        P(("dp", "ctx"), None),
        P(("dp", "ctx"), None),
    )
    out_specs = (P(("dp", "ctx"), "tp"), P(("dp", "ctx", "tp"), None))
    return jax.shard_map(
        per_device, mesh=mesh, in_specs=in_specs, out_specs=out_specs, check_vma=False
    )
```

```python
import functools
import math

import jax
import jax.numpy as jnp
from jax import lax
from jax.experimental import pallas as pl
from jax.experimental.pallas import tpu as pltpu
from jax.sharding import PartitionSpec as P

HEAD = 128


def rms_scale(proj_rows, norm_gain):
    inverse = lax.rsqrt(jnp.mean(proj_rows * proj_rows, axis=1, keepdims=True) + 1e-06)
    return (proj_rows * inverse * norm_gain).astype(jnp.bfloat16)


def routed_plan(
    queries,
    keys,
    values,
    out_weight,
    norm_gain,
    expert_gate,
    expert_up,
    expert_down,
    expert_ids,
    route_weights,
):
    ctx_count = lax.axis_size("ctx")
    tp_count = lax.axis_size("tp")
    ctx_index = lax.axis_index("ctx")
    tp_index = lax.axis_index("tp")
    block_rows = queries.shape[0]
    local_heads = queries.shape[1] // HEAD
    kv_local = keys.shape[1] // HEAD
    group_size = local_heads // kv_local
    query_grid = queries.reshape(block_rows, kv_local, group_size, HEAD)
    query_pos = ctx_index * block_rows + jnp.arange(block_rows, dtype=jnp.int32)
    last_query = ctx_index * block_rows + block_rows - 1
    score_scale = HEAD ** (-0.5)

    def key_step(state_now, key_part, value_part, first_key):
        running_max, row_total, accum = state_now
        key_count = key_part.shape[0]
        key_grid = key_part.reshape(key_count, kv_local, HEAD)
        value_grid = value_part.reshape(key_count, kv_local, HEAD)
        scores = (
            jnp.einsum("tkgd,ukd->kgtu", query_grid, key_grid, preferred_element_type=jnp.float32)
            * score_scale
        )
        key_pos = first_key + jnp.arange(key_count, dtype=jnp.int32)
        allowed = key_pos[None, :] <= query_pos[:, None]
        new_max = jnp.maximum(running_max, jnp.max(jnp.where(allowed, scores, -1e30), axis=3))
        key_weights = jnp.where(allowed, jnp.exp(scores - new_max[..., None]), 0.0)
        rescale = jnp.exp(running_max - new_max)
        row_total = row_total * rescale + jnp.sum(key_weights, axis=3)
        update = jnp.einsum(
            "kgtu,ukd->kgtd",
            key_weights.astype(jnp.bfloat16),
            value_grid,
            preferred_element_type=jnp.float32,
        )
        accum = accum * rescale[..., None] + update
        return (new_max, row_total, accum)

    initial = (
        jnp.full((kv_local, group_size, block_rows), -1e30, jnp.float32),
        jnp.zeros((kv_local, group_size, block_rows), jnp.float32),
        jnp.zeros((kv_local, group_size, block_rows, HEAD), jnp.float32),
    )
    running_state = initial
    key_rows = lax.all_gather(keys, "ctx", axis=0, tiled=True)
    value_rows = lax.all_gather(values, "ctx", axis=0, tiled=True)
    key_count = key_rows.shape[0]
    sub_rows = math.gcd(key_count, 512)

    def sub_step(partial_value, sub_index):
        offset = sub_index * sub_rows
        key_part = lax.dynamic_slice_in_dim(key_rows, offset, sub_rows, 0)
        value_part = lax.dynamic_slice_in_dim(value_rows, offset, sub_rows, 0)
        updated = lax.cond(
            offset <= last_query,
            lambda state_now: key_step(state_now, key_part, value_part, offset),
            lambda state_now: state_now,
            partial_value,
        )
        return (updated, None)

    running_state, unused = lax.scan(
        sub_step, running_state, jnp.arange(key_count // sub_rows, dtype=jnp.int32)
    )
    final_max, row_total, accum = running_state
    attended = (
        (accum / row_total[..., None])
        .transpose(2, 0, 1, 3)
        .reshape(block_rows, local_heads * HEAD)
        .astype(jnp.bfloat16)
    )
    own_proj = lax.psum_scatter(
        jnp.dot(attended, out_weight, preferred_element_type=jnp.float32).astype(jnp.bfloat16),
        "tp",
        scatter_dimension=0,
        tiled=True,
    ).astype(jnp.float32)
    normed = lax.all_gather(rms_scale(own_proj, norm_gain), "tp", axis=0, tiled=True)
    top_count = expert_ids.shape[1]
    capacity = block_rows * top_count // (ctx_count * tp_count) * 3 // 2
    slot_total = ctx_count * capacity
    is_mine = expert_ids % tp_count == tp_index
    target_ctx = expert_ids // tp_count
    flat_target = target_ctx.reshape(-1)
    flat_mine = is_mine.reshape(-1)
    to_target = (
        flat_target[:, None] == jnp.arange(ctx_count, dtype=jnp.int32)[None, :]
    ) & flat_mine[:, None]
    running = jnp.cumsum(to_target.astype(jnp.int32), axis=0) - 1
    position = jnp.sum(jnp.where(to_target, running, 0), axis=1)
    slot_id = jnp.where(flat_mine, flat_target * capacity + position, -1).reshape(
        block_rows, top_count
    )
    slot_match = slot_id[:, :, None] == jnp.arange(slot_total, dtype=jnp.int32)[None, None, :]
    dispatch_map = jnp.any(slot_match, axis=1).astype(jnp.bfloat16)
    outgoing = jnp.einsum(
        "ts,td->sd", dispatch_map, normed, preferred_element_type=jnp.float32
    ).astype(jnp.bfloat16)
    outgoing = outgoing.reshape(ctx_count, capacity, normed.shape[1])
    route_share = route_weights / jnp.sum(route_weights, axis=1, keepdims=True)
    mix_weights = jnp.sum(jnp.where(slot_match, route_share[:, :, None], 0.0), axis=1)
    mix_high = mix_weights.astype(jnp.bfloat16)
    mix_low = (mix_weights - mix_high.astype(jnp.float32)).astype(jnp.bfloat16)
    arrived = lax.all_to_all(outgoing, "ctx", split_axis=0, concat_axis=0, tiled=True)
    source_count, item_count, features = arrived.shape
    flattened = arrived.reshape(source_count * item_count, features)
    gate_proj = jnp.dot(flattened, expert_gate[0], preferred_element_type=jnp.float32)
    up_proj = jnp.dot(flattened, expert_up[0], preferred_element_type=jnp.float32)
    activated = (jax.nn.silu(gate_proj) * up_proj).astype(jnp.bfloat16)
    expert_out = jnp.dot(activated, expert_down[0], preferred_element_type=jnp.float32).astype(
        jnp.bfloat16
    )
    expert_out = expert_out.reshape(source_count, item_count, features)
    returned = lax.all_to_all(expert_out, "ctx", split_axis=0, concat_axis=0, tiled=True)
    returned_flat = returned.reshape(slot_total, returned.shape[2])
    high_part = jnp.dot(mix_high, returned_flat, preferred_element_type=jnp.float32)
    expert_mix = lax.psum_scatter(
        (high_part + jnp.dot(mix_low, returned_flat, preferred_element_type=jnp.float32)).astype(
            jnp.bfloat16
        ),
        "tp",
        scatter_dimension=0,
        tiled=True,
    ).astype(jnp.float32)
    layer_out = (own_proj + expert_mix).astype(jnp.bfloat16)
    return (attended, layer_out)


F32, BF16 = jnp.float32, jnp.bfloat16
VMEM_SPEC = pl.BlockSpec(memory_space=pltpu.VMEM)
HBM_SPEC = pl.BlockSpec(memory_space=pltpu.HBM)
HIDDEN_SCORE = -1e30
MIB = 1 << 20


def swap(rows, axis, offset):
    count = lax.axis_size(axis)
    return lax.ppermute(rows, axis, [(i, i ^ offset) for i in range(count)])


def call(kernel, outs, operands, scratch=(), flops=0, moved=0, limit=16 * MIB, from_hbm=0):
    operands = [
        pltpu.with_memory_space_constraint(x, pltpu.HBM) if i < from_hbm else x
        for i, x in enumerate(operands)
    ]
    return pl.pallas_call(
        kernel,
        out_shape=outs,
        in_specs=[HBM_SPEC] * from_hbm + [VMEM_SPEC] * (len(operands) - from_hbm),
        out_specs=[VMEM_SPEC] * len(outs),
        scratch_shapes=scratch,
        compiler_params=pltpu.CompilerParams(vmem_limit_bytes=limit),
        cost_estimate=pl.CostEstimate(flops=max(flops, 1024), bytes_accessed=1024, transcendentals=0),
    )(*operands)


def own_block_kernel(tp_count, *refs):
    sources, (q_ref, max_ref, total_ref, acc_ref, *mix_refs) = refs[:5], refs[5:-5]
    k_ref, v_ref, ids_ref, weights_ref, arrived = refs[-5:]
    targets = (q_ref, k_ref, v_ref, ids_ref, weights_ref)
    copies = [
        pltpu.make_async_copy(source, target, arrived.at[i])
        for i, (source, target) in enumerate(zip(sources, targets))
    ]
    for copy in copies:
        copy.start()
    for copy in copies:
        copy.wait()
    ctx_index, tp_index = lax.axis_index("ctx"), lax.axis_index("tp")
    block_rows = q_ref.shape[0]
    kv_local = k_ref.shape[1] // HEAD
    group_size = q_ref.shape[1] // k_ref.shape[1]
    key_pos = lax.broadcasted_iota(jnp.int32, (block_rows, block_rows), 0)
    query_pos = lax.broadcasted_iota(jnp.int32, (block_rows, block_rows), 1)
    for g in range(kv_local):
        key_rows = k_ref[:, g * HEAD : (g + 1) * HEAD]
        value_cols = v_ref[:, g * HEAD : (g + 1) * HEAD].astype(F32).T.astype(BF16)
        for h in range(g * group_size, (g + 1) * group_size):
            lanes = slice(h * HEAD, (h + 1) * HEAD)
            scores = lax.dot_general(
                key_rows, q_ref[:, lanes], (((1,), (1,)), ((), ())), preferred_element_type=F32
            )
            scores = jnp.where(key_pos <= query_pos, scores * HEAD ** (-0.5), HIDDEN_SCORE)
            top = jnp.max(scores, axis=0, keepdims=True)
            weights = jnp.exp(scores - top)
            max_ref[h : h + 1, :] = top
            total_ref[h : h + 1, :] = jnp.sum(weights, axis=0, keepdims=True)
            acc_ref[h] = jnp.dot(value_cols, weights.astype(BF16), preferred_element_type=F32)
    share = weights_ref[...] / jnp.sum(weights_ref[...], axis=0, keepdims=True)
    for d, mix_ref in enumerate(mix_refs):
        expert = (ctx_index ^ d) * tp_count + tp_index
        mix_ref[...] = jnp.sum(jnp.where(ids_ref[...] == expert, share, 0.0), axis=0, keepdims=True)


def other_blocks_kernel(tp_count, others, *refs):
    w_ref, q_ref, max_ref, total_ref, acc_ref = refs[:5]
    k_refs, v_refs = refs[5 : 5 + others], refs[5 + others : 5 + 2 * others]
    att_ref, *piece_refs = refs[5 + 2 * others : -1]
    scratch = refs[-1]
    ctx_index, tp_index = lax.axis_index("ctx"), lax.axis_index("tp")
    block_rows = q_ref.shape[0]
    kv_local = k_refs[0].shape[1] // HEAD
    group_size = q_ref.shape[1] // k_refs[0].shape[1]
    hide = [
        jnp.where((ctx_index ^ d) < ctx_index, 0.0, HIDDEN_SCORE) for d in range(1, others + 1)
    ]
    for g in range(kv_local):
        kv_lanes = slice(g * HEAD, (g + 1) * HEAD)
        key_rows = jnp.concatenate([r[:, kv_lanes] for r in k_refs], axis=0)
        value_rows = jnp.concatenate([r[:, kv_lanes] for r in v_refs], axis=0)
        value_cols = value_rows.astype(F32).T.astype(BF16)
        for h in range(g * group_size, (g + 1) * group_size):
            lanes = slice(h * HEAD, (h + 1) * HEAD)
            scores = lax.dot_general(
                key_rows, q_ref[:, lanes], (((1,), (1,)), ((), ())), preferred_element_type=F32
            )
            scores = jnp.concatenate(
                [
                    scores[i * block_rows : (i + 1) * block_rows] * HEAD ** (-0.5) + hide[i]
                    for i in range(others)
                ],
                axis=0,
            )
            old = max_ref[h : h + 1, :]
            top = jnp.maximum(old, jnp.max(scores, axis=0, keepdims=True))
            weights = jnp.exp(scores - top)
            rescale = jnp.exp(old - top)
            total = total_ref[h : h + 1, :] * rescale + jnp.sum(weights, axis=0, keepdims=True)
            accum = acc_ref[h] * rescale + jnp.dot(
                value_cols, weights.astype(BF16), preferred_element_type=F32
            )
            att_ref[:, lanes] = (accum * (1.0 / total)).T.astype(BF16)
    piece_rows = block_rows // tp_count
    scratch[...] = jnp.dot(att_ref[...], w_ref[...], preferred_element_type=F32)
    for d in range(tp_count):
        start = pl.multiple_of((tp_index ^ d) * piece_rows, piece_rows)
        piece_refs[d][...] = scratch[pl.ds(start, piece_rows), :].astype(piece_refs[d].dtype)


def norm_kernel(ctx_count, gain_ref, *refs):
    mix_refs, parts = refs[:ctx_count], refs[ctx_count:-6]
    proj_ref, normed_ref, column_ref = refs[-3:]
    proj = parts[0][...]
    for part in parts[1:]:
        proj = proj + part[...].astype(F32)
    proj_ref[...] = proj
    inverse = lax.rsqrt(jnp.mean(proj * proj, axis=1, keepdims=True) + 1e-06)
    normed_ref[...] = (proj * inverse * gain_ref[...]).astype(BF16)
    column_ref[...] = jnp.concatenate([r[...] for r in mix_refs], axis=0).T


def expert_kernel(offsets, *refs):
    count = len(refs) // 2 - 2
    token_refs, out_refs = refs[:count], refs[-count:]
    column_ref, gate_ref, up_ref, down_ref = refs[count : count + 4]
    rows = token_refs[0].shape[0]
    tokens = jnp.concatenate([r[...] for r in token_refs], axis=0)
    gate_proj = jnp.dot(tokens, gate_ref[0], preferred_element_type=F32)
    up_proj = jnp.dot(tokens, up_ref[0], preferred_element_type=F32)
    activated = (gate_proj / (1.0 + jnp.exp(-gate_proj)) * up_proj).astype(BF16)
    out = jnp.dot(activated, down_ref[0], preferred_element_type=F32)
    partners = count // len(offsets)
    for i, out_ref in enumerate(out_refs):
        start = pl.multiple_of((lax.axis_index("tp") ^ offsets[i // partners]) * rows, rows)
        mix = column_ref[pl.ds(start, rows), i % partners : i % partners + 1]
        out_ref[...] = (out[i * rows : (i + 1) * rows] * mix).astype(out_ref.dtype)


def sum_kernel(*refs):
    total = refs[0][...].astype(F32)
    for ref in refs[1:-1]:
        total = total + ref[...].astype(F32)
    refs[-1][...] = total.astype(refs[-1].dtype)


def dense_plan(
    queries,
    keys,
    values,
    out_weight,
    norm_gain,
    expert_gate,
    expert_up,
    expert_down,
    expert_ids,
    route_weights,
):
    ctx_count = lax.axis_size("ctx")
    tp_count = lax.axis_size("tp")
    block_rows, width = queries.shape
    heads = width // HEAD
    piece_rows = block_rows // tp_count
    features = out_weight.shape[1]
    shape = jax.ShapeDtypeStruct

    far_k, far_v = swap(keys, "ctx", 2), swap(values, "ctx", 2)
    near_k, near_v = swap(keys, "ctx", 1), swap(values, "ctx", 1)
    queries, top, total, accum, *mixes = call(
        functools.partial(own_block_kernel, tp_count),
        [shape((block_rows, width), BF16)]
        + [shape((heads, block_rows), F32)] * 2
        + [shape((heads, HEAD, block_rows), F32)]
        + [shape((1, block_rows), F32)] * ctx_count,
        (queries, keys, values, expert_ids.T, route_weights.T),
        scratch=[
            pltpu.VMEM(keys.shape, BF16),
            pltpu.VMEM(values.shape, BF16),
            pltpu.VMEM(expert_ids.T.shape, jnp.int32),
            pltpu.VMEM(route_weights.T.shape, F32),
            pltpu.SemaphoreType.DMA((5,)),
        ],
        flops=5 * 10**9,
        from_hbm=5,
    )
    far_k, far_v, top = lax.optimization_barrier((far_k, far_v, top))
    ks = [near_k, far_k, swap(far_k, "ctx", 1)]
    vs = [near_v, far_v, swap(far_v, "ctx", 1)]
    piece = shape((piece_rows, features), BF16)
    piece32 = shape((piece_rows, features), F32)
    attended, *partials = call(
        functools.partial(other_blocks_kernel, tp_count, ctx_count - 1),
        [shape((block_rows, width), BF16), piece32] + [piece] * (tp_count - 1),
        (out_weight, queries, top, total, accum, *ks, *vs),
        scratch=[pltpu.VMEM((block_rows, features), F32)],
    )

    arrived = [swap(partials[d], "tp", d) for d in (2, 3, 1)]
    mixes = mixes[:1] + [swap(mixes[d], "ctx", d) for d in range(1, ctx_count)]
    own_proj, normed, columns = call(
        functools.partial(norm_kernel, ctx_count),
        [piece32, piece, shape((block_rows, ctx_count), F32)],
        (
            norm_gain.reshape(1, features),
            *mixes,
            partials[0],
            *arrived,
            expert_gate,
            expert_up,
            expert_down,
        ),
    )

    def after(values, *earlier):
        return lax.optimization_barrier((tuple(values), earlier))[0]

    def work(group, tokens):
        found = call(
            functools.partial(expert_kernel, group),
            [piece32, piece, piece32, piece] * len(group),
            (*tokens, columns, expert_gate, expert_up, expert_down),
                )
        return [found[4 * i : 4 * i + 4] for i in range(len(group))]

    def spread(rows, far):
        return [rows, swap(rows, "ctx", 1), far, swap(far, "ctx", 1)]

    def gather_results(out):
        out0, out1, out2, out3 = out
        got0, got2 = swap(out1, "ctx", 1), swap(out3, "ctx", 1)
        (far_part,) = call(sum_kernel, [piece], (out2, got2))
        return [out0, got0, far_part]

    def send_back(parts, d):
        out0, got0, far_part = parts
        parts = [out0, got0, swap(far_part, "ctx", 2)]
        if not d:
            return parts
        (tp_part,) = call(sum_kernel, [piece], parts)
        return [swap(tp_part, "tp", d)]

    rows2, rows1 = swap(normed, "tp", 2), swap(normed, "tp", 1)
    far0 = swap(normed, "ctx", 2)
    far1 = swap(rows1, "ctx", 2)
    far2 = swap(rows2, "ctx", 2)
    rows3 = swap(rows2, "tp", 1)
    rows0, far0, rows1, far1 = after((normed, far0, rows1, far1), rows2)
    tokens = spread(rows1, far1) + spread(rows2, far2)
    far3 = swap(rows3, "ctx", 2)
    tokens = after(tokens, rows3)
    out1, out2 = work((1, 2), tokens)
    parts2 = gather_results(out2)
    rows0, far0, rows3, far3 = after((rows0, far0, rows3, far3), out1[0])
    tokens = spread(rows0, far0) + spread(rows3, far3)
    tokens = after(tokens, parts2[2])
    back2 = swap(parts2[2], "ctx", 2)
    out0, out3 = work((0, 3), tokens)
    (back2,) = after((back2,), out3[2])
    (tp2,) = call(sum_kernel, [piece], (*parts2[:2], back2), flops=10**9)
    ret2 = swap(tp2, "tp", 2)
    out3 = [out3[0], out3[1], *after((out3[2],), tp2), out3[3]]
    parts3 = gather_results(out3)
    back3 = swap(parts3[2], "ctx", 2)
    out1 = [out1[0], out1[1], *after((out1[2],), parts3[2]), out1[3]]
    parts1 = gather_results(out1)
    back1 = swap(parts1[2], "ctx", 2)
    (back3,) = after((back3,), parts1[2])
    (tp3,) = call(sum_kernel, [piece], (*parts3[:2], back3))
    ret3 = swap(tp3, "tp", 3)
    (back1,) = after((back1,), tp3, ret2)
    (tp1,) = call(sum_kernel, [piece], (*parts1[:2], back1))
    ret1 = swap(tp1, "tp", 1)
    results = [own_proj, ret1, ret2, ret3]
    out0 = [out0[0], out0[1], *after((out0[2],), parts1[2]), out0[3]]
    parts0 = gather_results(out0)
    (far_part0,) = after((parts0[2],), back1)
    results += send_back([*parts0[:2], far_part0], 0)
    (layer_out,) = call(sum_kernel, [piece], results)
    return (attended, layer_out)


def per_device(*arguments):
    ctx_count, tp_count = lax.axis_size("ctx"), lax.axis_size("tp")
    top_count = arguments[8].shape[1]
    if ctx_count == 4 and tp_count == 4 and ctx_count * tp_count <= 2 * top_count:
        return dense_plan(*arguments)
    return routed_plan(*arguments)


def solution(mesh):
    in_specs = (
        P(("dp", "ctx"), "tp"),
        P(("dp", "ctx"), "tp"),
        P(("dp", "ctx"), "tp"),
        P("tp", None),
        P(),
        P(("ctx", "tp"), None, None),
        P(("ctx", "tp"), None, None),
        P(("ctx", "tp"), None, None),
        P(("dp", "ctx"), None),
        P(("dp", "ctx"), None),
    )
    out_specs = (P(("dp", "ctx"), "tp"), P(("dp", "ctx", "tp"), None))
    return jax.shard_map(
        per_device, mesh=mesh, in_specs=in_specs, out_specs=out_specs, check_vma=False
    )
```

```python
import functools
import math

import jax
import jax.numpy as jnp
from jax import lax
from jax.experimental import pallas as pl
from jax.experimental.pallas import tpu as pltpu
from jax.sharding import PartitionSpec as P

HEAD = 128


def rms_scale(proj_rows, norm_gain):
    inverse = lax.rsqrt(jnp.mean(proj_rows * proj_rows, axis=1, keepdims=True) + 1e-06)
    return (proj_rows * inverse * norm_gain).astype(jnp.bfloat16)


def routed_plan(
    queries,
    keys,
    values,
    out_weight,
    norm_gain,
    expert_gate,
    expert_up,
    expert_down,
    expert_ids,
    route_weights,
):
    ctx_count = lax.axis_size("ctx")
    tp_count = lax.axis_size("tp")
    ctx_index = lax.axis_index("ctx")
    tp_index = lax.axis_index("tp")
    block_rows = queries.shape[0]
    local_heads = queries.shape[1] // HEAD
    kv_local = keys.shape[1] // HEAD
    group_size = local_heads // kv_local
    query_grid = queries.reshape(block_rows, kv_local, group_size, HEAD)
    query_pos = ctx_index * block_rows + jnp.arange(block_rows, dtype=jnp.int32)
    last_query = ctx_index * block_rows + block_rows - 1
    score_scale = HEAD ** (-0.5)

    def key_step(state_now, key_part, value_part, first_key):
        running_max, row_total, accum = state_now
        key_count = key_part.shape[0]
        key_grid = key_part.reshape(key_count, kv_local, HEAD)
        value_grid = value_part.reshape(key_count, kv_local, HEAD)
        scores = (
            jnp.einsum("tkgd,ukd->kgtu", query_grid, key_grid, preferred_element_type=jnp.float32)
            * score_scale
        )
        key_pos = first_key + jnp.arange(key_count, dtype=jnp.int32)
        allowed = key_pos[None, :] <= query_pos[:, None]
        new_max = jnp.maximum(running_max, jnp.max(jnp.where(allowed, scores, -1e30), axis=3))
        key_weights = jnp.where(allowed, jnp.exp(scores - new_max[..., None]), 0.0)
        rescale = jnp.exp(running_max - new_max)
        row_total = row_total * rescale + jnp.sum(key_weights, axis=3)
        update = jnp.einsum(
            "kgtu,ukd->kgtd",
            key_weights.astype(jnp.bfloat16),
            value_grid,
            preferred_element_type=jnp.float32,
        )
        accum = accum * rescale[..., None] + update
        return (new_max, row_total, accum)

    initial = (
        jnp.full((kv_local, group_size, block_rows), -1e30, jnp.float32),
        jnp.zeros((kv_local, group_size, block_rows), jnp.float32),
        jnp.zeros((kv_local, group_size, block_rows, HEAD), jnp.float32),
    )
    running_state = initial
    key_rows = lax.all_gather(keys, "ctx", axis=0, tiled=True)
    value_rows = lax.all_gather(values, "ctx", axis=0, tiled=True)
    key_count = key_rows.shape[0]
    sub_rows = math.gcd(key_count, 512)

    def sub_step(partial_value, sub_index):
        offset = sub_index * sub_rows
        key_part = lax.dynamic_slice_in_dim(key_rows, offset, sub_rows, 0)
        value_part = lax.dynamic_slice_in_dim(value_rows, offset, sub_rows, 0)
        updated = lax.cond(
            offset <= last_query,
            lambda state_now: key_step(state_now, key_part, value_part, offset),
            lambda state_now: state_now,
            partial_value,
        )
        return (updated, None)

    running_state, unused = lax.scan(
        sub_step, running_state, jnp.arange(key_count // sub_rows, dtype=jnp.int32)
    )
    final_max, row_total, accum = running_state
    attended = (
        (accum / row_total[..., None])
        .transpose(2, 0, 1, 3)
        .reshape(block_rows, local_heads * HEAD)
        .astype(jnp.bfloat16)
    )
    own_proj = lax.psum_scatter(
        jnp.dot(attended, out_weight, preferred_element_type=jnp.float32).astype(jnp.bfloat16),
        "tp",
        scatter_dimension=0,
        tiled=True,
    ).astype(jnp.float32)
    normed = lax.all_gather(rms_scale(own_proj, norm_gain), "tp", axis=0, tiled=True)
    top_count = expert_ids.shape[1]
    capacity = block_rows * top_count // (ctx_count * tp_count) * 3 // 2
    slot_total = ctx_count * capacity
    is_mine = expert_ids % tp_count == tp_index
    target_ctx = expert_ids // tp_count
    flat_target = target_ctx.reshape(-1)
    flat_mine = is_mine.reshape(-1)
    to_target = (
        flat_target[:, None] == jnp.arange(ctx_count, dtype=jnp.int32)[None, :]
    ) & flat_mine[:, None]
    running = jnp.cumsum(to_target.astype(jnp.int32), axis=0) - 1
    position = jnp.sum(jnp.where(to_target, running, 0), axis=1)
    slot_id = jnp.where(flat_mine, flat_target * capacity + position, -1).reshape(
        block_rows, top_count
    )
    slot_match = slot_id[:, :, None] == jnp.arange(slot_total, dtype=jnp.int32)[None, None, :]
    dispatch_map = jnp.any(slot_match, axis=1).astype(jnp.bfloat16)
    outgoing = jnp.einsum(
        "ts,td->sd", dispatch_map, normed, preferred_element_type=jnp.float32
    ).astype(jnp.bfloat16)
    outgoing = outgoing.reshape(ctx_count, capacity, normed.shape[1])
    route_share = route_weights / jnp.sum(route_weights, axis=1, keepdims=True)
    mix_weights = jnp.sum(jnp.where(slot_match, route_share[:, :, None], 0.0), axis=1)
    mix_high = mix_weights.astype(jnp.bfloat16)
    mix_low = (mix_weights - mix_high.astype(jnp.float32)).astype(jnp.bfloat16)
    arrived = lax.all_to_all(outgoing, "ctx", split_axis=0, concat_axis=0, tiled=True)
    source_count, item_count, features = arrived.shape
    flattened = arrived.reshape(source_count * item_count, features)
    gate_proj = jnp.dot(flattened, expert_gate[0], preferred_element_type=jnp.float32)
    up_proj = jnp.dot(flattened, expert_up[0], preferred_element_type=jnp.float32)
    activated = (jax.nn.silu(gate_proj) * up_proj).astype(jnp.bfloat16)
    expert_out = jnp.dot(activated, expert_down[0], preferred_element_type=jnp.float32).astype(
        jnp.bfloat16
    )
    expert_out = expert_out.reshape(source_count, item_count, features)
    returned = lax.all_to_all(expert_out, "ctx", split_axis=0, concat_axis=0, tiled=True)
    returned_flat = returned.reshape(slot_total, returned.shape[2])
    high_part = jnp.dot(mix_high, returned_flat, preferred_element_type=jnp.float32)
    expert_mix = lax.psum_scatter(
        (high_part + jnp.dot(mix_low, returned_flat, preferred_element_type=jnp.float32)).astype(
            jnp.bfloat16
        ),
        "tp",
        scatter_dimension=0,
        tiled=True,
    ).astype(jnp.float32)
    layer_out = (own_proj + expert_mix).astype(jnp.bfloat16)
    return (attended, layer_out)


F32, BF16 = jnp.float32, jnp.bfloat16
VMEM_SPEC = pl.BlockSpec(memory_space=pltpu.VMEM)
HBM_SPEC = pl.BlockSpec(memory_space=pltpu.HBM)
HIDDEN_SCORE = -1e30
MIB = 1 << 20


def swap(rows, axis, offset):
    count = lax.axis_size(axis)
    return lax.ppermute(rows, axis, [(i, i ^ offset) for i in range(count)])


def call(kernel, outs, operands, scratch=(), flops=0, moved=0, limit=16 * MIB, from_hbm=0):
    operands = [
        pltpu.with_memory_space_constraint(x, pltpu.HBM) if i < from_hbm else x
        for i, x in enumerate(operands)
    ]
    return pl.pallas_call(
        kernel,
        out_shape=outs,
        in_specs=[HBM_SPEC] * from_hbm + [VMEM_SPEC] * (len(operands) - from_hbm),
        out_specs=[VMEM_SPEC] * len(outs),
        scratch_shapes=scratch,
        compiler_params=pltpu.CompilerParams(vmem_limit_bytes=limit),
        cost_estimate=pl.CostEstimate(flops=max(flops, 1024), bytes_accessed=1024, transcendentals=0),
    )(*operands)


def own_heads(heads, q_ref, k_ref, v_ref, max_ref, total_ref, acc_ref):
    block_rows = q_ref.shape[0]
    group_size = q_ref.shape[1] // k_ref.shape[1]
    key_pos = lax.broadcasted_iota(jnp.int32, (block_rows, block_rows), 0)
    query_pos = lax.broadcasted_iota(jnp.int32, (block_rows, block_rows), 1)
    value_cols = {}
    for i, h in enumerate(heads):
        kv_lanes = slice(h // group_size * HEAD, (h // group_size + 1) * HEAD)
        if h // group_size not in value_cols:
            value_cols[h // group_size] = v_ref[:, kv_lanes].astype(F32).T.astype(BF16)
        scores = lax.dot_general(
            k_ref[:, kv_lanes],
            q_ref[:, h * HEAD : (h + 1) * HEAD],
            (((1,), (1,)), ((), ())),
            preferred_element_type=F32,
        )
        scores = jnp.where(key_pos <= query_pos, scores * HEAD ** (-0.5), HIDDEN_SCORE)
        top = jnp.max(scores, axis=0, keepdims=True)
        weights = jnp.exp(scores - top)
        max_ref[i : i + 1, :] = top
        total_ref[i : i + 1, :] = jnp.sum(weights, axis=0, keepdims=True)
        acc_ref[i] = jnp.dot(
            value_cols[h // group_size], weights.astype(BF16), preferred_element_type=F32
        )


def first_kernel(tp_count, heads, *refs):
    sources, (q_ref, k_ref, v_ref, max_ref, total_ref, acc_ref, *mix_refs) = refs[:5], refs[5:-3]
    ids_ref, weights_ref, arrived = refs[-3:]
    targets = (q_ref, k_ref, v_ref, ids_ref, weights_ref)
    copies = [
        pltpu.make_async_copy(source, target, arrived.at[i])
        for i, (source, target) in enumerate(zip(sources, targets))
    ]
    for copy in copies:
        copy.start()
    for copy in copies:
        copy.wait()
    ctx_index, tp_index = lax.axis_index("ctx"), lax.axis_index("tp")
    own_heads(heads, q_ref, k_ref, v_ref, max_ref, total_ref, acc_ref)
    share = weights_ref[...] / jnp.sum(weights_ref[...], axis=0, keepdims=True)
    for d, mix_ref in enumerate(mix_refs):
        expert = (ctx_index ^ d) * tp_count + tp_index
        mix_ref[...] = jnp.sum(jnp.where(ids_ref[...] == expert, share, 0.0), axis=0, keepdims=True)


def other_blocks_kernel(tp_count, others, *refs):
    w_ref, q_ref = refs[:2]
    states = (refs[2:5], refs[5:8])
    k_refs, v_refs = refs[8 : 8 + others], refs[8 + others : 8 + 2 * others]
    att_ref, *piece_refs = refs[8 + 2 * others : -1]
    scratch = refs[-1]
    ctx_index, tp_index = lax.axis_index("ctx"), lax.axis_index("tp")
    block_rows = q_ref.shape[0]
    kv_local = k_refs[0].shape[1] // HEAD
    group_size = q_ref.shape[1] // k_refs[0].shape[1]
    hide = [
        jnp.where((ctx_index ^ d) < ctx_index, 0.0, HIDDEN_SCORE) for d in range(1, others + 1)
    ]
    for g in range(kv_local):
        kv_lanes = slice(g * HEAD, (g + 1) * HEAD)
        key_rows = jnp.concatenate([r[:, kv_lanes] for r in k_refs], axis=0)
        value_rows = jnp.concatenate([r[:, kv_lanes] for r in v_refs], axis=0)
        value_cols = value_rows.astype(F32).T.astype(BF16)
        for h in range(g * group_size, (g + 1) * group_size):
            lanes = slice(h * HEAD, (h + 1) * HEAD)
            scores = lax.dot_general(
                key_rows, q_ref[:, lanes], (((1,), (1,)), ((), ())), preferred_element_type=F32
            )
            scores = jnp.concatenate(
                [
                    scores[j * block_rows : (j + 1) * block_rows] * HEAD ** (-0.5) + hide[j]
                    for j in range(others)
                ],
                axis=0,
            )
            half = states[0][0].shape[0]
            max_ref, total_ref, acc_ref = states[h // half]
            i = h % half
            old = max_ref[i : i + 1, :]
            top = jnp.maximum(old, jnp.max(scores, axis=0, keepdims=True))
            weights = jnp.exp(scores - top)
            rescale = jnp.exp(old - top)
            total = total_ref[i : i + 1, :] * rescale + jnp.sum(weights, axis=0, keepdims=True)
            accum = acc_ref[i] * rescale + jnp.dot(
                value_cols, weights.astype(BF16), preferred_element_type=F32
            )
            att_ref[:, lanes] = (accum * (1.0 / total)).T.astype(BF16)
    piece_rows = block_rows // tp_count
    scratch[...] = jnp.dot(att_ref[...], w_ref[...], preferred_element_type=F32)
    for d in range(tp_count):
        start = pl.multiple_of((tp_index ^ d) * piece_rows, piece_rows)
        piece_refs[d][...] = scratch[pl.ds(start, piece_rows), :].astype(piece_refs[d].dtype)


def norm_kernel(ctx_count, gain_ref, *refs):
    mix_refs, parts = refs[:ctx_count], refs[ctx_count:-6]
    proj_ref, normed_ref, column_ref = refs[-3:]
    proj = parts[0][...]
    for part in parts[1:]:
        proj = proj + part[...].astype(F32)
    proj_ref[...] = proj
    inverse = lax.rsqrt(jnp.mean(proj * proj, axis=1, keepdims=True) + 1e-06)
    normed_ref[...] = (proj * inverse * gain_ref[...]).astype(BF16)
    column_ref[...] = jnp.concatenate([r[...] for r in mix_refs], axis=0).T


def expert_kernel(offsets, *refs):
    count = len(refs) // 2 - 2
    token_refs, out_refs = refs[:count], refs[-count:]
    column_ref, gate_ref, up_ref, down_ref = refs[count : count + 4]
    rows = token_refs[0].shape[0]
    tokens = jnp.concatenate([r[...] for r in token_refs], axis=0)
    gate_proj = jnp.dot(tokens, gate_ref[0], preferred_element_type=F32)
    up_proj = jnp.dot(tokens, up_ref[0], preferred_element_type=F32)
    activated = (gate_proj / (1.0 + jnp.exp(-gate_proj)) * up_proj).astype(BF16)
    out = jnp.dot(activated, down_ref[0], preferred_element_type=F32)
    partners = count // len(offsets)
    for i, out_ref in enumerate(out_refs):
        start = pl.multiple_of((lax.axis_index("tp") ^ offsets[i // partners]) * rows, rows)
        mix = column_ref[pl.ds(start, rows), i % partners : i % partners + 1]
        out_ref[...] = (out[i * rows : (i + 1) * rows] * mix).astype(out_ref.dtype)


def sum_kernel(*refs):
    total = refs[0][...].astype(F32)
    for ref in refs[1:-1]:
        total = total + ref[...].astype(F32)
    refs[-1][...] = total.astype(refs[-1].dtype)


def dense_plan(
    queries,
    keys,
    values,
    out_weight,
    norm_gain,
    expert_gate,
    expert_up,
    expert_down,
    expert_ids,
    route_weights,
):
    ctx_count = lax.axis_size("ctx")
    tp_count = lax.axis_size("tp")
    block_rows, width = queries.shape
    heads = width // HEAD
    piece_rows = block_rows // tp_count
    features = out_weight.shape[1]
    shape = jax.ShapeDtypeStruct

    far_k, far_v = swap(keys, "ctx", 2), swap(values, "ctx", 2)
    near_k, near_v = swap(keys, "ctx", 1), swap(values, "ctx", 1)
    half = heads // 2
    state = [shape((half, block_rows), F32)] * 2 + [shape((half, HEAD, block_rows), F32)]
    q, k, v, *found = call(
        functools.partial(first_kernel, tp_count, range(half)),
        [shape((block_rows, width), BF16), shape(keys.shape, BF16), shape(values.shape, BF16)]
        + state
        + [shape((1, block_rows), F32)] * ctx_count,
        (queries, keys, values, expert_ids.T, route_weights.T),
        scratch=[
            pltpu.VMEM(expert_ids.T.shape, jnp.int32),
            pltpu.VMEM(route_weights.T.shape, F32),
            pltpu.SemaphoreType.DMA((5,)),
        ],
        flops=5 * 10**9,
        from_hbm=5,
    )
    first, mixes = found[:3], found[3:]
    far_k, far_v, first[0] = lax.optimization_barrier((far_k, far_v, first[0]))
    second = call(functools.partial(own_heads, range(half, heads)), state, (q, k, v))
    ks = [near_k, far_k, swap(far_k, "ctx", 1)]
    vs = [near_v, far_v, swap(far_v, "ctx", 1)]
    piece = shape((piece_rows, features), BF16)
    piece32 = shape((piece_rows, features), F32)
    attended, *partials = call(
        functools.partial(other_blocks_kernel, tp_count, ctx_count - 1),
        [shape((block_rows, width), BF16), piece32] + [piece] * (tp_count - 1),
        (out_weight, q, *first, *second, *ks, *vs),
        scratch=[pltpu.VMEM((block_rows, features), F32)],
    )

    arrived = [swap(partials[d], "tp", d) for d in (2, 3, 1)]
    mixes = mixes[:1] + [swap(mixes[d], "ctx", d) for d in range(1, ctx_count)]
    own_proj, normed, columns = call(
        functools.partial(norm_kernel, ctx_count),
        [piece32, piece, shape((block_rows, ctx_count), F32)],
        (
            norm_gain.reshape(1, features),
            *mixes,
            partials[0],
            *arrived,
            expert_gate,
            expert_up,
            expert_down,
        ),
    )

    def after(values, *earlier):
        return lax.optimization_barrier((tuple(values), earlier))[0]

    def work(group, tokens):
        found = call(
            functools.partial(expert_kernel, group),
            [piece32, piece, piece32, piece] * len(group),
            (*tokens, columns, expert_gate, expert_up, expert_down),
                )
        return [found[4 * i : 4 * i + 4] for i in range(len(group))]

    def spread(rows, far):
        return [rows, swap(rows, "ctx", 1), far, swap(far, "ctx", 1)]

    def gather_results(out):
        out0, out1, out2, out3 = out
        got0, got2 = swap(out1, "ctx", 1), swap(out3, "ctx", 1)
        (far_part,) = call(sum_kernel, [piece], (out2, got2))
        return [out0, got0, far_part]

    def send_back(parts, d):
        out0, got0, far_part = parts
        parts = [out0, got0, swap(far_part, "ctx", 2)]
        if not d:
            return parts
        (tp_part,) = call(sum_kernel, [piece], parts)
        return [swap(tp_part, "tp", d)]

    rows2, rows1 = swap(normed, "tp", 2), swap(normed, "tp", 1)
    far0 = swap(normed, "ctx", 2)
    far1 = swap(rows1, "ctx", 2)
    far2 = swap(rows2, "ctx", 2)
    rows3 = swap(rows2, "tp", 1)
    rows0, far0, rows1, far1 = after((normed, far0, rows1, far1), rows2)
    tokens = spread(rows1, far1) + spread(rows2, far2)
    far3 = swap(rows3, "ctx", 2)
    tokens = after(tokens, rows3)
    out1, out2 = work((1, 2), tokens)
    parts2 = gather_results(out2)
    rows0, far0, rows3, far3 = after((rows0, far0, rows3, far3), out1[0])
    tokens = spread(rows0, far0) + spread(rows3, far3)
    tokens = after(tokens, parts2[2])
    back2 = swap(parts2[2], "ctx", 2)
    out0, out3 = work((0, 3), tokens)
    (back2,) = after((back2,), out3[2])
    (tp2,) = call(sum_kernel, [piece], (*parts2[:2], back2), flops=10**9)
    ret2 = swap(tp2, "tp", 2)
    out3 = [out3[0], out3[1], *after((out3[2],), tp2), out3[3]]
    parts3 = gather_results(out3)
    back3 = swap(parts3[2], "ctx", 2)
    out1 = [out1[0], out1[1], *after((out1[2],), parts3[2]), out1[3]]
    parts1 = gather_results(out1)
    back1 = swap(parts1[2], "ctx", 2)
    (back3,) = after((back3,), parts1[2])
    (tp3,) = call(sum_kernel, [piece], (*parts3[:2], back3))
    ret3 = swap(tp3, "tp", 3)
    (back1,) = after((back1,), tp3, ret2)
    (tp1,) = call(sum_kernel, [piece], (*parts1[:2], back1))
    ret1 = swap(tp1, "tp", 1)
    results = [own_proj, ret1, ret2, ret3]
    out0 = [out0[0], out0[1], *after((out0[2],), parts1[2]), out0[3]]
    parts0 = gather_results(out0)
    (far_part0,) = after((parts0[2],), back1)
    results += send_back([*parts0[:2], far_part0], 0)
    (layer_out,) = call(sum_kernel, [piece], results)
    return (attended, layer_out)


def per_device(*arguments):
    ctx_count, tp_count = lax.axis_size("ctx"), lax.axis_size("tp")
    top_count = arguments[8].shape[1]
    if ctx_count == 4 and tp_count == 4 and ctx_count * tp_count <= 2 * top_count:
        return dense_plan(*arguments)
    return routed_plan(*arguments)


def solution(mesh):
    in_specs = (
        P(("dp", "ctx"), "tp"),
        P(("dp", "ctx"), "tp"),
        P(("dp", "ctx"), "tp"),
        P("tp", None),
        P(),
        P(("ctx", "tp"), None, None),
        P(("ctx", "tp"), None, None),
        P(("ctx", "tp"), None, None),
        P(("dp", "ctx"), None),
        P(("dp", "ctx"), None),
    )
    out_specs = (P(("dp", "ctx"), "tp"), P(("dp", "ctx", "tp"), None))
    return jax.shard_map(
        per_device, mesh=mesh, in_specs=in_specs, out_specs=out_specs, check_vma=False
    )
```
